256 devices in a mesh: row: 32 (over y, x, core), col: 8 (over z).
Axes of the slice: x: 4, y: 4, z: 8, core: 2. Of those that a mesh axis runs over, the one named last changes fastest.
Arguments:
- gen_points: bfloat16 [16384, 128], P('row'), may hold values from -1.796875 to 1.796875
- ref_points: bfloat16 [65536, 128], P('col'), may hold values from -1.796875 to 1.796875
- gen_mass: float32 [16384], P('row'), may hold values from 0.25 to 4
- ref_mass: float32 [65536], P('col'), may hold values from 0.25 to 4
Outputs:
- sample_side_multiplier: float32 [16384], P('row')
- anchor_side_multiplier: float32 [65536], P('col')
- gen_grad: float32 [16384, 128], P('row')
The draws below stay inside these ranges and needn't reach their ends.
All inputs are finite; a program needn't handle non-finite values.
Results may differ from the reference program's by a relative error of at most 0.0015.
Values sent between devices are 32-bit elements; how exact they have to be, the bound alone decides.
A program may use at most 64 MiB of HBM per device.

```python
import math
import jax
import jax.numpy as jnp
from jax import lax

DIM = 128
ITERS = 2
SAMPLE_SIZE = 16384
NR = 65536


def shard_levels(stream_key, dims, shards, smallest, high):
    def one(position, shards_of):
        heights = jax.random.uniform(jax.random.fold_in(jax.random.fold_in(stream_key, 6), position), (shards_of,), jnp.float32, smallest / len(shards), high / len(shards))
        return jnp.repeat(jnp.exp(heights), dims[position] // shards_of).reshape((-1,) + (1,) * (len(dims) - position - 1))

    loudness = one(*shards[0])
    for cut in shards[1:]:
        loudness = loudness * one(*cut)
    return loudness


def normal_values(key, dims, width, bound, split=(), held_as=jnp.bfloat16):
    entries = jax.random.normal(key, dims, jnp.float32) * width
    if len(split) > 0:
        entries = shard_levels(key, dims, split, -0.22, 0.18) * entries
    return jnp.clip(entries, min=-bound, max=bound).astype(held_as)


def setup_inputs(seed: int = 0) -> dict:
    keys = jax.random.split(jax.random.key(seed), 5)
    return {
        "gen_points": normal_values(keys[0], (SAMPLE_SIZE, DIM), 0.3, 1.796875, ((0, 32),)),
        "ref_points": normal_values(keys[1], (NR, DIM), 0.3, 1.796875, ((0, 8),)),
        "gen_mass": jnp.clip(jnp.exp(math.log(4.0) - 2.7725887 * jax.random.uniform(keys[2], (SAMPLE_SIZE,), jnp.float32) ** shard_levels(keys[2], (SAMPLE_SIZE,), ((0, 32),), -0.2, 0.2)), 0.25, 4.0),
        "ref_mass": jnp.clip(jnp.exp(math.log(4.0) - 2.7725887 * jax.random.uniform(keys[3], (NR,), jnp.float32) ** shard_levels(keys[3], (NR,), ((0, 8),), -0.2, 0.2)), 0.25, 4.0),
    }


smoothing_epsilon = 0.05


def reference(gen_points, ref_points, gen_mass, ref_mass):
    gen_wide = gen_points.astype(jnp.float32)
    ref_wide = ref_points.astype(jnp.float32)
    sq_gen = 0.5 * jnp.sum(gen_wide * gen_wide, axis=1)
    sq_ref = 0.5 * jnp.sum(ref_wide * ref_wide, axis=1)
    logarithmic_left_marginal = jnp.log(gen_mass) - jnp.log(jnp.sum(gen_mass))
    logarithmic_right_marginal = jnp.log(ref_mass) - jnp.log(jnp.sum(ref_mass))
    row_block = math.gcd(SAMPLE_SIZE, 256)
    col_block = math.gcd(NR, 256)
    gen_blocks = gen_points.reshape(SAMPLE_SIZE // row_block, row_block, DIM)
    sqg_blocks = sq_gen.reshape(SAMPLE_SIZE // row_block, row_block)
    loga_blocks = logarithmic_left_marginal.reshape(SAMPLE_SIZE // row_block, row_block)
    ref_blocks = ref_points.reshape(NR // col_block, col_block, DIM)
    sqr_blocks = sq_ref.reshape(NR // col_block, col_block)
    logb_blocks = logarithmic_right_marginal.reshape(NR // col_block, col_block)

    def update_gen(anchor_side_multiplier):
        def one(items):
            embedding_points, squared_norms = items
            pairwise_distance_matrix = squared_norms[:, None] + sq_ref[None, :] - jnp.dot(embedding_points, ref_points.T, preferred_element_type=jnp.float32)
            gibbs_exponent = logarithmic_right_marginal[None, :] + (anchor_side_multiplier[None, :] - pairwise_distance_matrix) / smoothing_epsilon
            current_largest_exponent = jnp.max(gibbs_exponent, axis=1)
            current_partial_sum = jnp.sum(jnp.exp(gibbs_exponent - current_largest_exponent[:, None]), axis=1)
            return -smoothing_epsilon * (current_largest_exponent + jnp.log(current_partial_sum))
        return lax.map(one, (gen_blocks, sqg_blocks)).reshape(SAMPLE_SIZE)

    def update_ref(sample_side_multiplier):
        def one(items):
            embedding_points, squared_norms, logarithmic_gibbs_entries = items
            pairwise_distance_matrix = sq_gen[:, None] + squared_norms[None, :] - jnp.dot(gen_points, embedding_points.T, preferred_element_type=jnp.float32)
            gibbs_exponent = logarithmic_left_marginal[:, None] + (sample_side_multiplier[:, None] - pairwise_distance_matrix) / smoothing_epsilon
            current_largest_exponent = jnp.max(gibbs_exponent, axis=0)
            current_partial_sum = jnp.sum(jnp.exp(gibbs_exponent - current_largest_exponent[None, :]), axis=0)
            return -smoothing_epsilon * (current_largest_exponent + jnp.log(current_partial_sum))
        return lax.map(one, (ref_blocks, sqr_blocks, logb_blocks)).reshape(NR)

    anchor_side_multiplier = jnp.zeros((NR,), jnp.float32)
    sample_side_multiplier = jnp.zeros((SAMPLE_SIZE,), jnp.float32)
    for repeat in range(ITERS):
        sample_side_multiplier = update_gen(anchor_side_multiplier)
        anchor_side_multiplier = update_ref(sample_side_multiplier)
    fpot_blocks = sample_side_multiplier.reshape(SAMPLE_SIZE // row_block, row_block)

    def gradient(items):
        embedding_points, squared_norms, logarithmic_gibbs_entries, row_side_multiplier = items
        pairwise_distance_matrix = squared_norms[:, None] + sq_ref[None, :] - jnp.dot(embedding_points, ref_points.T, preferred_element_type=jnp.float32)
        optimal_plan_matrix = SAMPLE_SIZE * jnp.exp(logarithmic_gibbs_entries[:, None] + logarithmic_right_marginal[None, :] + (row_side_multiplier[:, None] + anchor_side_multiplier[None, :] - pairwise_distance_matrix) / smoothing_epsilon)
        mass_row = jnp.sum(optimal_plan_matrix, axis=1)
        pulled = jnp.dot(optimal_plan_matrix.astype(jnp.bfloat16), ref_points, preferred_element_type=jnp.float32)
        return mass_row[:, None] * embedding_points.astype(jnp.float32) - pulled

    gen_grad = lax.map(gradient, (gen_blocks, sqg_blocks, loga_blocks, fpot_blocks)).reshape(SAMPLE_SIZE, DIM)
    return sample_side_multiplier, anchor_side_multiplier, gen_grad
```

```python
import math

import jax
import jax.numpy as jnp
from jax import lax
from jax.experimental import pallas as pl
from jax.experimental.pallas import tpu as pltpu
from jax.sharding import PartitionSpec as P

smoothing_epsilon = 0.05
SCALE = 1.0 / (smoothing_epsilon * math.log(2.0))
LANES = 128
SUB = 8
LOWEST = -3.0e38
f32 = jnp.float32
MESH = pl.DeviceIdType.MESH

CHUNK = 64
TILE1 = 1024
TILE2 = 1024
GROUPS3 = 16
GROUPS4 = 4
TILE5 = 2048
ROWS5 = 128


def scores(a, b):
    return lax.dot_general(a, b, (((1,), (1,)), ((), ())), preferred_element_type=f32)


def lane_cols(group):
    return pl.ds(pl.multiple_of(group * LANES, LANES), LANES)


def total(v):
    return jnp.sum(jnp.sum(v, axis=0, keepdims=True), axis=1, keepdims=True)


def kernel(
    nrow, ncol, x, y, gm, rm, f_out, g_out, grad_out,
    R, MH, beta, acc_a, acc_b, lanes_u,
    zs1, zr1, cs2, cr2, gs2, gr2, zs3, zr3, cs4, cr4, gs4, gr4, pull, part, pr5, done,
    send_sem, recv_sem,
):
    rows, width = x.shape
    cols = y.shape[0]
    row_blocks = rows // LANES
    groups = cols // LANES
    per = groups // nrow
    r = lax.axis_index("row")
    c = lax.axis_index("col")

    def row_peer(s):
        return lax.rem(r + s, nrow)

    def col_peer(s):
        return lax.rem(c + s, ncol)

    barrier = pltpu.get_barrier_semaphore()

    def greet_row(s, carry):
        pl.semaphore_signal(barrier, inc=1, device_id={"row": row_peer(s)}, device_id_type=MESH)
        return carry

    def greet_col(s, carry):
        pl.semaphore_signal(barrier, inc=1, device_id={"col": col_peer(s)}, device_id_type=MESH)
        return carry

    lax.fori_loop(1, nrow, greet_row, 0)
    lax.fori_loop(1, ncol, greet_col, 0)

    def exchange(phase, count, peer, axis, source, target):
        def one(s, carry):
            k = peer(s)
            pltpu.make_async_remote_copy(
                src_ref=source(k),
                dst_ref=target,
                send_sem=send_sem.at[phase],
                recv_sem=recv_sem.at[phase],
                device_id={axis: k},
                device_id_type=MESH,
            ).start()
            return carry

        lax.fori_loop(1, count, one, 0)

    def arrived(phase, whole):
        pltpu.make_async_copy(whole, whole, recv_sem.at[phase]).wait()

    def left(phase, whole):
        pltpu.make_async_copy(whole, whole, send_sem.at[phase]).wait()

    def norms(b, carry):
        wide = y[pl.ds(pl.multiple_of(b * 1024, 1024), 1024), :].astype(f32)
        squares = wide * wide
        for k in range(8):
            half = jnp.sum(squares[k * LANES:(k + 1) * LANES].T, axis=0, keepdims=True)
            beta[pl.ds(b * 8 + k, 1), :] = half
        return carry

    lax.fori_loop(0, cols // 1024, norms, 0)
    log_ref = jnp.log2(rm[...])
    beta[...] = log_ref - (0.5 * SCALE) * beta[...]

    acc_a[...] = jnp.full(acc_a.shape, LOWEST, f32)
    acc_b[...] = jnp.zeros(acc_b.shape, f32)
    n1 = TILE1 // LANES

    def pass1(t, carry):
        block = scores(x[...], y[pl.ds(pl.multiple_of(t * TILE1, TILE1), TILE1), :])
        bias = [beta[pl.ds(t * n1 + k, 1), :] for k in range(n1)]
        for i in range(0, rows, SUB):
            e = [block[i:i + SUB, k * LANES:(k + 1) * LANES] * SCALE + bias[k] for k in range(n1)]
            old = acc_a[i:i + SUB, :]
            top = e[0]
            for v in e[1:]:
                top = jnp.maximum(top, v)
            top = jnp.maximum(top, old)
            s = acc_b[i:i + SUB, :] * jnp.exp2(old - top)
            for v in e:
                s = s + jnp.exp2(v - top)
            acc_a[i:i + SUB, :] = top
            acc_b[i:i + SUB, :] = s
        return carry

    lax.fori_loop(0, cols // TILE1, pass1, 0)

    for k in range(row_blocks):
        part_rows = slice(k * LANES, (k + 1) * LANES)
        v = (acc_a[part_rows, :] + jnp.log2(acc_b[part_rows, :])).T
        top = jnp.max(v, axis=0, keepdims=True)
        zs1[k:k + 1, :] = top + jnp.log2(jnp.sum(jnp.exp2(v - top), axis=0, keepdims=True))
    zs1[row_blocks:, :] = jnp.broadcast_to(total(rm[...]), (SUB - row_blocks, LANES))

    pl.semaphore_wait(barrier, (nrow - 1) + (ncol - 1))

    exchange(0, ncol, col_peer, "col", lambda k: zs1, zr1.at[c])
    zr1[c] = zs1[...]
    arrived(0, zr1.at[pl.ds(0, ncol - 1)])
    v = zr1[...]
    top = jnp.max(v, axis=0)
    lse = top + jnp.log2(jnp.sum(jnp.exp2(v - top[None]), axis=0))
    ref_total = jnp.sum(v, axis=0)[row_blocks:row_blocks + 1, :]
    row_lse = lse[:row_blocks, :] - jnp.log2(ref_total)
    alpha = jnp.log2(gm[...]) - row_lse
    for k in range(row_blocks):
        lanes_u[k * LANES:(k + 1) * LANES, :] = jnp.broadcast_to(alpha[k:k + 1, :], (LANES, LANES)).T

    n2 = TILE2 // LANES
    cs2[:, per:, :] = jnp.broadcast_to(total(gm[...])[None], (nrow, cs2.shape[1] - per, LANES))

    def pass2(t, carry):
        block = scores(x[...], y[pl.ds(pl.multiple_of(t * TILE2, TILE2), TILE2), :])
        bias = [beta[pl.ds(t * n2 + k, 1), :] for k in range(n2)]
        tops = [jnp.full((SUB, LANES), LOWEST, f32) for _ in range(n2)]
        sums = [jnp.zeros((SUB, LANES), f32) for _ in range(n2)]
        for q in range(rows // CHUNK):
            span = range(q * CHUNK, (q + 1) * CHUNK, SUB)
            al = [lanes_u[i:i + SUB, :] for i in span]
            for k in range(n2):
                e = [block[i:i + SUB, k * LANES:(k + 1) * LANES] * SCALE + a for i, a in zip(span, al)]
                top = tops[k]
                for v in e:
                    top = jnp.maximum(top, v)
                s = sums[k] * jnp.exp2(tops[k] - top)
                for i, v in zip(span, e):
                    z = jnp.exp2(v - top)
                    R[i:i + SUB, lane_cols(t * n2 + k)] = z
                    s = s + z
                tops[k] = top
                sums[k] = s
                MH[q * SUB:(q + 1) * SUB, lane_cols(t * n2 + k)] = top + bias[k]
        for k in range(n2):
            top = jnp.max(tops[k], axis=0, keepdims=True)
            s = jnp.sum(sums[k] * jnp.exp2(tops[k] - top), axis=0, keepdims=True)
            cs2[t * (n2 // per) + k // per, k % per:k % per + 1, :] = top + jnp.log2(s) + bias[k]
        return carry

    lax.fori_loop(0, cols // TILE2, pass2, 0)

    exchange(1, nrow, row_peer, "row", lambda k: cs2.at[k], cr2.at[r])
    cr2[r] = cs2[r]
    arrived(1, cr2.at[pl.ds(0, nrow - 1)])
    v = cr2[...]
    top = jnp.max(v, axis=0)
    lse = top + jnp.log2(jnp.sum(jnp.exp2(v - top[None]), axis=0))
    gs2[:per, :] = lse[:per, :]
    gen_total = jnp.sum(v, axis=0)[per:per + 1, :]
    exchange(2, nrow, row_peer, "row", lambda k: gs2, gr2.at[r])
    gr2[r] = gs2[...]
    arrived(2, gr2.at[pl.ds(0, nrow - 1)])

    def weigh(b, carry):
        for h in range(per):
            g = b * per + h
            ref_share = rm[pl.ds(g, 1), :] / ref_total
            col = gr2[b, h:h + 1, :]
            v = MH[:, lane_cols(g)]
            MH[:, lane_cols(g)] = jnp.exp2(v - col) * ref_share
        return carry

    lax.fori_loop(0, nrow, weigh, 0, unroll=4)

    acc_a[...] = jnp.zeros(acc_a.shape, f32)

    def pass3(t, carry):
        for q in range(rows // CHUNK):
            w = [MH[q * SUB:(q + 1) * SUB, lane_cols(t * GROUPS3 + k)] for k in range(GROUPS3)]
            for i in range(q * CHUNK, (q + 1) * CHUNK, SUB):
                even = acc_a[i:i + SUB, :]
                odd = jnp.zeros((SUB, LANES), f32)
                for k in range(GROUPS3):
                    v = R[i:i + SUB, lane_cols(t * GROUPS3 + k)] * w[k]
                    if k % 2:
                        odd = odd + v
                    else:
                        even = even + v
                acc_a[i:i + SUB, :] = even + odd
        return carry

    lax.fori_loop(0, groups // GROUPS3, pass3, 0)
    for k in range(row_blocks):
        zs3[k:k + 1, :] = jnp.sum(acc_a[k * LANES:(k + 1) * LANES, :].T, axis=0, keepdims=True)
    exchange(3, ncol, col_peer, "col", lambda k: zs3, zr3.at[c])
    zr3[c] = zs3[...]
    arrived(3, zr3.at[pl.ds(0, ncol - 1)])
    u = gm[...] / (gen_total * jnp.sum(zr3[...], axis=0))
    for k in range(row_blocks):
        lanes_u[k * LANES:(k + 1) * LANES, :] = jnp.broadcast_to(u[k:k + 1, :], (LANES, LANES)).T
        wide = x[k * LANES:(k + 1) * LANES, :].astype(f32)
        half = 0.5 * jnp.sum((wide * wide).T, axis=0, keepdims=True)
        f_out[k:k + 1, :] = half + (jnp.log2(u[k:k + 1, :]) - row_lse[k:k + 1, :]) * (1.0 / SCALE)

    def pass4(t, carry):
        sums = [jnp.zeros((SUB, LANES), f32) for _ in range(GROUPS4)]
        for q in range(rows // CHUNK):
            inner = [jnp.zeros((SUB, LANES), f32) for _ in range(GROUPS4)]
            for i in range(q * CHUNK, (q + 1) * CHUNK, SUB):
                a = lanes_u[i:i + SUB, :]
                for k in range(GROUPS4):
                    inner[k] = inner[k] + R[i:i + SUB, lane_cols(t * GROUPS4 + k)] * a
            for k in range(GROUPS4):
                sums[k] = sums[k] + inner[k] * MH[q * SUB:(q + 1) * SUB, lane_cols(t * GROUPS4 + k)]
        for k in range(GROUPS4):
            cs4[t * (GROUPS4 // per) + k // per, k % per:k % per + 1, :] = jnp.sum(sums[k], axis=0, keepdims=True)
        return carry

    lax.fori_loop(0, groups // GROUPS4, pass4, 0)

    exchange(4, nrow, row_peer, "row", lambda k: cs4.at[k], cr4.at[r])
    cr4[r] = cs4[r]
    arrived(4, cr4.at[pl.ds(0, nrow - 1)])
    plan_cols = jnp.sum(cr4[...], axis=0)
    for h in range(per):
        gs4[h:h + 1, :] = rm[pl.ds(r * per + h, 1), :] / (ref_total * plan_cols[h:h + 1, :])
    exchange(5, nrow, row_peer, "row", lambda k: gs4, gr4.at[r])
    gr4[r] = gs4[...]
    arrived(5, gr4.at[pl.ds(0, nrow - 1)])

    acc_a[...] = jnp.zeros(acc_a.shape, f32)
    pull[...] = jnp.zeros(pull.shape, f32)
    lanes_u[...] = lanes_u[...] * float(rows * nrow)
    n5 = TILE5 // LANES

    def pass5(t, carry):
        points = y[pl.ds(pl.multiple_of(t * TILE5, TILE5), TILE5), :]
        ratio = [gr4[t * (n5 // per) + k // per, k % per:k % per + 1, :] for k in range(n5)]
        for i0 in range(0, rows, ROWS5):
            low = [[] for _ in range(n5)]
            for q in range(i0 // CHUNK, (i0 + ROWS5) // CHUNK):
                w = [MH[q * SUB:(q + 1) * SUB, lane_cols(t * n5 + k)] * ratio[k] for k in range(n5)]
                for i in range(q * CHUNK, (q + 1) * CHUNK, SUB):
                    a = lanes_u[i:i + SUB, :]
                    mass = acc_a[i:i + SUB, :]
                    for k in range(n5):
                        p = (R[i:i + SUB, lane_cols(t * n5 + k)] * w[k]) * a
                        mass = mass + p
                        low[k].append(p)
                    acc_a[i:i + SUB, :] = mass
            plan_low = jnp.concatenate(
                [jnp.concatenate(v, axis=0).astype(jnp.bfloat16) for v in low], axis=1
            )
            pull[i0:i0 + ROWS5, :] += jnp.dot(plan_low, points, preferred_element_type=f32)
        return carry

    lax.fori_loop(0, cols // TILE5, pass5, 0)

    mass_row = jnp.sum(acc_a[...], axis=1, keepdims=True)
    part[...] = mass_row * x[...].astype(f32) - pull[...]

    share = rows // ncol

    def rows_of(k):
        return pl.ds(pl.multiple_of(k * share, share), share)

    exchange(6, ncol, col_peer, "col", lambda k: part.at[rows_of(k)], pr5.at[c])
    pr5[c] = part[rows_of(c), :]

    log_total = jnp.log2(gen_total)
    for b in range(nrow):
        for h in range(per):
            g = b * per + h
            g_out[g:g + 1, :] = (
                (log_total + jnp.log2(rm[g:g + 1, :]) - gr2[b, h:h + 1, :])
                + jnp.log2(gr4[b, h:h + 1, :])
            ) * (1.0 / SCALE)

    arrived(6, pr5.at[pl.ds(0, ncol - 1)])
    done[rows_of(c), :] = jnp.sum(pr5[...], axis=0)
    exchange(7, ncol, col_peer, "col", lambda k: done.at[rows_of(c)], done.at[rows_of(c)])
    arrived(7, done.at[pl.ds(0, rows - share)])
    grad_out[...] = done[...]

    left(0, zr1.at[pl.ds(0, ncol - 1)])
    left(1, cr2.at[pl.ds(0, nrow - 1)])
    left(2, gr2.at[pl.ds(0, nrow - 1)])
    left(3, zr3.at[pl.ds(0, ncol - 1)])
    left(4, cr4.at[pl.ds(0, nrow - 1)])
    left(5, gr4.at[pl.ds(0, nrow - 1)])
    left(6, pr5.at[pl.ds(0, ncol - 1)])
    left(7, done.at[pl.ds(0, rows - share)])


def local(nrow, ncol, gen_points, ref_points, gen_mass, ref_mass):
    rows, width = gen_points.shape
    cols = ref_points.shape[0]
    row_blocks = rows // LANES
    groups = cols // LANES
    per = groups // nrow
    chunks = rows // CHUNK
    vmem = pl.BlockSpec(memory_space=pltpu.VMEM)

    def buf(*shape):
        return pltpu.VMEM(shape, f32)

    def body(*refs):
        kernel(nrow, ncol, *refs)

    f, g, grad = pl.pallas_call(
        body,
        out_shape=(
            jax.ShapeDtypeStruct((row_blocks, LANES), f32),
            jax.ShapeDtypeStruct((groups, LANES), f32),
            jax.ShapeDtypeStruct((rows, width), f32),
        ),
        in_specs=[vmem] * 4,
        out_specs=(vmem, vmem, vmem),
        scratch_shapes=[
            buf(rows, cols), buf(chunks * SUB, cols), buf(groups, LANES),
            buf(rows, LANES), buf(rows, LANES), buf(rows, LANES),
            buf(SUB, LANES), buf(ncol, SUB, LANES),
            buf(nrow, 2 * per, LANES), buf(nrow, 2 * per, LANES),
            buf(per, LANES), buf(nrow, per, LANES),
            buf(row_blocks, LANES), buf(ncol, row_blocks, LANES),
            buf(nrow, per, LANES), buf(nrow, per, LANES),
            buf(per, LANES), buf(nrow, per, LANES),
            buf(rows, width), buf(rows, width), buf(ncol, rows // ncol, width), buf(rows, width),
            pltpu.SemaphoreType.DMA((8,)),
            pltpu.SemaphoreType.DMA((8,)),
        ],
        compiler_params=pltpu.CompilerParams(
            collective_id=0, has_side_effects=True, vmem_limit_bytes=56 * 2**20
        ),
        name="sinkhorn",
    )(gen_points, ref_points, gen_mass.reshape(row_blocks, LANES), ref_mass.reshape(groups, LANES))
    return f.reshape(rows), g.reshape(cols), grad


def solution(mesh):
    nrow, ncol = mesh.shape["row"], mesh.shape["col"]

    def run(*args):
        return local(nrow, ncol, *args)

    return jax.shard_map(
        run,
        mesh=mesh,
        in_specs=(P("row", None), P("col", None), P("row"), P("col")),
        out_specs=(P("row"), P("col"), P("row", None)),
        check_vma=False,
    )
```

```python
import math

import jax
import jax.numpy as jnp
from jax import lax
from jax.experimental import pallas as pl
from jax.experimental.pallas import tpu as pltpu
from jax.sharding import PartitionSpec as P

smoothing_epsilon = 0.05
SCALE = 1.0 / (smoothing_epsilon * math.log(2.0))
LANES = 128
SUB = 8
LOWEST = -3.0e38
f32 = jnp.float32
MESH = pl.DeviceIdType.MESH

CHUNK = 64
TILE1 = 2048
TILE2 = 2048
GROUPS3 = 16
GROUPS4 = 4
TILE5 = 2048
ROWS5 = 128
PARTS = 2


def scores(a, b):
    return lax.dot_general(a, b, (((1,), (1,)), ((), ())), preferred_element_type=f32)


def lane_cols(group):
    return pl.ds(pl.multiple_of(group * LANES, LANES), LANES)


def tile_rows(t):
    return pl.ds(pl.multiple_of(t * SUB, SUB), SUB)


def total(v):
    return jnp.sum(jnp.sum(v, axis=0, keepdims=True), axis=1, keepdims=True)


def log_sum(v):
    top = jnp.max(v, axis=0)
    return top + jnp.log2(jnp.sum(jnp.exp2(v - top[None]), axis=0))


def kernel(
    nrow, ncol, x, y, gm, rm, f_out, g_out, grad_out,
    R, MH, TOP, SUM, beta, acc_a, acc_b, lanes_u, row_f,
    sa, ra, ca, ta, zs1, zr1, zs3, zr3,
    cs2, cr2, gs2, ag2, col2, cs4, cr4, gs4, ag4, col4,
    pull, part, pr5, done, send_sem, recv_sem,
):
    rows, width = x.shape
    cols = y.shape[0]
    row_blocks = rows // LANES
    groups = cols // LANES
    tiles = groups // SUB
    half_tiles = tiles // 2
    half_groups = groups // 2
    chips = nrow // 2
    part_rows = rows // PARTS
    part_blocks = part_rows // LANES
    r = lax.axis_index("row")
    c = lax.axis_index("col")
    core = lax.rem(r, 2)
    chip = r // 2
    partner = 2 * chip + (1 - core)
    own = core * half_tiles
    other = (1 - core) * half_tiles

    def chip_peer(s):
        return lax.rem(r + 2 * s, nrow)

    def col_peer(s):
        return lax.rem(c + s, ncol)

    barrier = pltpu.get_barrier_semaphore()

    def greet_row(s, carry):
        pl.semaphore_signal(barrier, inc=1, device_id={"row": chip_peer(s)}, device_id_type=MESH)
        return carry

    def greet_col(s, carry):
        pl.semaphore_signal(barrier, inc=1, device_id={"col": col_peer(s)}, device_id_type=MESH)
        return carry

    pl.semaphore_signal(barrier, inc=1, device_id={"row": partner}, device_id_type=MESH)
    lax.fori_loop(1, chips, greet_row, 0)
    lax.fori_loop(1, ncol, greet_col, 0)

    def send(phase, device, source, target):
        pltpu.make_async_remote_copy(
            src_ref=source,
            dst_ref=target,
            send_sem=send_sem.at[phase],
            recv_sem=recv_sem.at[phase],
            device_id=device,
            device_id_type=MESH,
        ).start()

    def to_chips(phase, source, target):
        def one(s, carry):
            send(phase, {"row": chip_peer(s)}, source, target)
            return carry

        lax.fori_loop(1, chips, one, 0)

    def to_cols(phase, source, target):
        def one(s, carry):
            k = col_peer(s)
            send(phase, {"col": k}, source(k), target)
            return carry

        lax.fori_loop(1, ncol, one, 0)

    def arrived(phase, whole):
        pltpu.make_async_copy(whole, whole, recv_sem.at[phase]).wait()

    def left(phase, whole):
        pltpu.make_async_copy(whole, whole, send_sem.at[phase]).wait()

    Z1, Z3, CORE2, CHIP2, BACK2, CORE4, CHIP4, BACK4, RS, AG, A1, A2 = (
        0, 2, 4, 8, 12, 13, 17, 21, 22, 26, 30, 31,
    )

    def norms(b, carry):
        wide = y[pl.ds(pl.multiple_of(b * 1024, 1024), 1024), :].astype(f32)
        squares = wide * wide
        for k in range(8):
            half = jnp.sum(squares[k * LANES:(k + 1) * LANES].T, axis=0, keepdims=True)
            beta[pl.ds(b * 8 + k, 1), :] = half
        return carry

    lax.fori_loop(0, cols // 1024, norms, 0)
    log_ref = jnp.log2(rm[...])
    beta[...] = log_ref - (0.5 * SCALE) * beta[...]
    zs1[...] = jnp.broadcast_to(total(rm[...])[None], zs1.shape)
    sa[...] = jnp.broadcast_to(total(gm[...]), sa.shape)

    acc_a[...] = jnp.full(acc_a.shape, LOWEST, f32)
    acc_b[...] = jnp.zeros(acc_b.shape, f32)
    n1 = TILE1 // LANES

    def pass1(h, t):
        block = scores(x[h * part_rows:(h + 1) * part_rows, :], y[pl.ds(pl.multiple_of(t * TILE1, TILE1), TILE1), :])
        bias = [beta[pl.ds(t * n1 + k, 1), :] for k in range(n1)]
        for i in range(0, part_rows, SUB):
            o = h * part_rows + i
            e = [block[i:i + SUB, k * LANES:(k + 1) * LANES] * SCALE + bias[k] for k in range(n1)]
            old = acc_a[o:o + SUB, :]
            top = e[0]
            for v in e[1:]:
                top = jnp.maximum(top, v)
            top = jnp.maximum(top, old)
            s = acc_b[o:o + SUB, :] * jnp.exp2(old - top)
            for v in e:
                s = s + jnp.exp2(v - top)
            acc_a[o:o + SUB, :] = top
            acc_b[o:o + SUB, :] = s

    for h in range(PARTS):
        def pass1_tile(t, carry, h=h):
            pass1(h, t)
            return carry

        lax.fori_loop(0, cols // TILE1, pass1_tile, 0)
        for k in range(part_blocks):
            o = (h * part_blocks + k) * LANES
            v = (acc_a[o:o + LANES, :] + jnp.log2(acc_b[o:o + LANES, :])).T
            top = jnp.max(v, axis=0, keepdims=True)
            zs1[h, k:k + 1, :] = top + jnp.log2(jnp.sum(jnp.exp2(v - top), axis=0, keepdims=True))
        if h == 0:
            pl.semaphore_wait(barrier, chips + ncol - 1)
            send(A1, {"row": partner}, sa, ra)
        to_cols(Z1 + h, lambda k: zs1.at[h], zr1.at[h, c])
        zr1[h, c] = zs1[h]

    n2 = TILE2 // LANES
    t2 = n2 // SUB

    def row_weights(v, h):
        for k in range(part_blocks):
            o = (h * part_blocks + k) * LANES
            lanes_u[o:o + LANES, :] = jnp.broadcast_to(v[k:k + 1, :], (LANES, LANES)).T

    def pass2(h, g0):
        block = scores(
            x[h * part_rows:(h + 1) * part_rows, :],
            y[pl.ds(pl.multiple_of(g0 * LANES, TILE2), TILE2), :],
        )
        bias = [beta[pl.ds(g0 + k, 1), :] for k in range(n2)]
        tops = [TOP[:, lane_cols(g0 + k)] if h else jnp.full((SUB, LANES), LOWEST, f32) for k in range(n2)]
        sums = [SUM[:, lane_cols(g0 + k)] if h else jnp.zeros((SUB, LANES), f32) for k in range(n2)]
        for q in range(part_rows // CHUNK):
            span = range(q * CHUNK, (q + 1) * CHUNK, SUB)
            o = h * part_rows
            al = [lanes_u[o + i:o + i + SUB, :] for i in span]
            hq = (h * (part_rows // CHUNK) + q) * SUB
            for k in range(n2):
                e = [block[i:i + SUB, k * LANES:(k + 1) * LANES] * SCALE + a for i, a in zip(span, al)]
                top = tops[k]
                for v in e:
                    top = jnp.maximum(top, v)
                s = sums[k] * jnp.exp2(tops[k] - top)
                for i, v in zip(span, e):
                    z = jnp.exp2(v - top)
                    R[o + i:o + i + SUB, lane_cols(g0 + k)] = z
                    s = s + z
                tops[k] = top
                sums[k] = s
                MH[hq:hq + SUB, lane_cols(g0 + k)] = top + bias[k]
        if h < PARTS - 1:
            for k in range(n2):
                TOP[:, lane_cols(g0 + k)] = tops[k]
                SUM[:, lane_cols(g0 + k)] = sums[k]
            return
        for k in range(n2):
            top = jnp.max(tops[k], axis=0, keepdims=True)
            s = jnp.sum(sums[k] * jnp.exp2(tops[k] - top), axis=0, keepdims=True)
            cs2[pl.ds(g0 + k, 1), :] = top + jnp.log2(s) + bias[k]

    def log_of_rows(h):
        arrived(Z1 + h, zr1.at[h, pl.ds(0, ncol - 1)])
        v = zr1[h]
        lse = log_sum(v)[:part_blocks, :]
        ref_total = jnp.sum(v, axis=0)[part_blocks:part_blocks + 1, :]
        row_lse = lse - jnp.log2(ref_total)
        block = slice(h * part_blocks, (h + 1) * part_blocks)
        row_f[block, :] = row_lse
        row_weights(jnp.log2(gm[block, :]) - row_lse, h)
        return ref_total

    for h in range(PARTS - 1):
        ref_total = log_of_rows(h)

        def pass2_tile(t, carry, h=h):
            pass2(h, t * n2)
            return carry

        lax.fori_loop(0, groups // n2, pass2_tile, 0)
    arrived(A1, ra)
    ca[...] = sa[...] + ra[...]
    to_chips(A2, ca, ta.at[chip])
    ta[chip] = ca[...]
    log_of_rows(PARTS - 1)

    def pass2_other(t, carry):
        g0 = other * SUB + t * n2
        pass2(PARTS - 1, g0)
        for j in range(t2):
            at = tile_rows(other + t * t2 + j)
            send(CORE2 + t * t2 + j, {"row": partner}, cs2.at[at], cr2.at[at])
        return carry

    def pass2_own(t, carry):
        g0 = own * SUB + t * n2
        pass2(PARTS - 1, g0)
        for j in range(t2):
            at = tile_rows(own + t * t2 + j)
            mine = tile_rows(t * t2 + j)
            arrived(CORE2 + t * t2 + j, cr2.at[at])
            a, b = cs2[at, :], cr2[at, :]
            top = jnp.maximum(a, b)
            both = top + jnp.log2(jnp.exp2(a - top) + jnp.exp2(b - top))
            gs2[mine, :] = both
            ag2[chip, mine, :] = both
            to_chips(CHIP2 + t * t2 + j, gs2.at[mine], ag2.at[chip, mine])
        return carry

    lax.fori_loop(0, half_groups // n2, pass2_other, 0)
    lax.fori_loop(0, half_groups // n2, pass2_own, 0)

    for j in range(half_tiles):
        mine = slice(j * SUB, (j + 1) * SUB)
        arrived(CHIP2 + j, ag2.at[pl.ds(0, chips - 1), mine])
        col2[tile_rows(own + j), :] = log_sum(ag2[:, mine, :])
    own_groups = pl.ds(pl.multiple_of(own * SUB, SUB), half_groups)
    other_groups = pl.ds(pl.multiple_of(other * SUB, SUB), half_groups)
    send(BACK2, {"row": partner}, col2.at[own_groups], col2.at[own_groups])

    def weigh(first):
        def one(j, carry):
            g = first * SUB + j
            ref_share = rm[pl.ds(g, 1), :] / ref_total
            MH[:, lane_cols(g)] = jnp.exp2(MH[:, lane_cols(g)] - col2[pl.ds(g, 1), :]) * ref_share
            return carry

        lax.fori_loop(0, half_groups, one, 0, unroll=4)

    def pass3(first, h):
        def tile(t, carry):
            g0 = first * SUB + t * GROUPS3
            for q in range(part_rows // CHUNK):
                hq = (h * (part_rows // CHUNK) + q) * SUB
                w = [MH[hq:hq + SUB, lane_cols(g0 + k)] for k in range(GROUPS3)]
                for i in range(h * part_rows + q * CHUNK, h * part_rows + (q + 1) * CHUNK, SUB):
                    even = acc_a[i:i + SUB, :]
                    odd = jnp.zeros((SUB, LANES), f32)
                    for k in range(GROUPS3):
                        v = R[i:i + SUB, lane_cols(g0 + k)] * w[k]
                        if k % 2:
                            odd = odd + v
                        else:
                            even = even + v
                    acc_a[i:i + SUB, :] = even + odd
            return carry

        lax.fori_loop(0, half_groups // GROUPS3, tile, 0)

    acc_a[...] = jnp.zeros(acc_a.shape, f32)
    weigh(own)
    for h in range(PARTS):
        pass3(own, h)
    arrived(BACK2, col2.at[other_groups])
    weigh(other)
    for h in range(PARTS):
        pass3(other, h)
        for k in range(part_blocks):
            o = (h * part_blocks + k) * LANES
            zs3[h, k:k + 1, :] = jnp.sum(acc_a[o:o + LANES, :].T, axis=0, keepdims=True)
        to_cols(Z3 + h, lambda k: zs3.at[h], zr3.at[h, c])
        zr3[h, c] = zs3[h]

    def pass4(h, g0):
        sums = [SUM[:, lane_cols(g0 + k)] if h else jnp.zeros((SUB, LANES), f32) for k in range(GROUPS4)]
        for q in range(part_rows // CHUNK):
            hq = (h * (part_rows // CHUNK) + q) * SUB
            inner = [jnp.zeros((SUB, LANES), f32) for _ in range(GROUPS4)]
            for i in range(h * part_rows + q * CHUNK, h * part_rows + (q + 1) * CHUNK, SUB):
                a = lanes_u[i:i + SUB, :]
                for k in range(GROUPS4):
                    inner[k] = inner[k] + R[i:i + SUB, lane_cols(g0 + k)] * a
            for k in range(GROUPS4):
                sums[k] = sums[k] + inner[k] * MH[hq:hq + SUB, lane_cols(g0 + k)]
        for k in range(GROUPS4):
            if h < PARTS - 1:
                SUM[:, lane_cols(g0 + k)] = sums[k]
            else:
                cs4[pl.ds(g0 + k, 1), :] = jnp.sum(sums[k], axis=0, keepdims=True)

    def scale_rows(h):
        arrived(Z3 + h, zr3.at[h, pl.ds(0, ncol - 1)])
        block = slice(h * part_blocks, (h + 1) * part_blocks)
        u = gm[block, :] / jnp.sum(zr3[h], axis=0)
        row_weights(u, h)
        row_f[block, :] = jnp.log2(u) - row_f[block, :]

    for h in range(PARTS - 1):
        scale_rows(h)

        def pass4_tile(t, carry, h=h):
            pass4(h, t * GROUPS4)
            return carry

        lax.fori_loop(0, groups // GROUPS4, pass4_tile, 0)
    scale_rows(PARTS - 1)

    def pass4_other(j, carry):
        for k in range(SUB // GROUPS4):
            pass4(PARTS - 1, (other + j) * SUB + k * GROUPS4)
        at = tile_rows(other + j)
        send(CORE4 + j, {"row": partner}, cs4.at[at], cr4.at[at])
        return carry

    def pass4_own(j, carry):
        for k in range(SUB // GROUPS4):
            pass4(PARTS - 1, (own + j) * SUB + k * GROUPS4)
        at = tile_rows(own + j)
        mine = tile_rows(j)
        arrived(CORE4 + j, cr4.at[at])
        both = cs4[at, :] + cr4[at, :]
        gs4[mine, :] = both
        ag4[chip, mine, :] = both
        to_chips(CHIP4 + j, gs4.at[mine], ag4.at[chip, mine])
        return carry

    lax.fori_loop(0, half_tiles, pass4_other, 0)
    lax.fori_loop(0, half_tiles, pass4_own, 0)

    arrived(A2, ta.at[pl.ds(0, chips - 1)])
    log_total = jnp.log2(jnp.sum(ta[...], axis=0)[0:1, :])
    for k in range(row_blocks):
        wide = x[k * LANES:(k + 1) * LANES, :].astype(f32)
        half = 0.5 * jnp.sum((wide * wide).T, axis=0, keepdims=True)
        f_out[k:k + 1, :] = half + (row_f[k:k + 1, :] - log_total) * (1.0 / SCALE)
    lanes_u[...] = lanes_u[...] * float(rows * nrow)
    acc_a[...] = jnp.zeros(acc_a.shape, f32)

    for j in range(half_tiles):
        mine = slice(j * SUB, (j + 1) * SUB)
        at = tile_rows(own + j)
        arrived(CHIP4 + j, ag4.at[pl.ds(0, chips - 1), mine])
        col4[at, :] = rm[at, :] / (ref_total * jnp.sum(ag4[:, mine, :], axis=0))
    send(BACK4, {"row": partner}, col4.at[own_groups], col4.at[own_groups])
    arrived(BACK4, col4.at[other_groups])

    n5 = TILE5 // LANES
    share = ROWS5 // ncol

    def pass5(b, carry):
        base = pl.multiple_of(b * ROWS5, ROWS5)
        pulled = jnp.zeros((ROWS5, width), f32)
        for t in range(cols // TILE5):
            low = [[] for _ in range(n5)]
            for q in range(ROWS5 // CHUNK):
                hq = pl.ds(pl.multiple_of(b * (ROWS5 // CHUNK * SUB) + q * SUB, SUB), SUB)
                w = [MH[hq, (t * n5 + k) * LANES:(t * n5 + k + 1) * LANES] * col4[t * n5 + k:t * n5 + k + 1, :]
                     for k in range(n5)]
                for i in range(q * CHUNK, (q + 1) * CHUNK, SUB):
                    at = pl.ds(pl.multiple_of(base + i, SUB), SUB)
                    a = lanes_u[at, :]
                    mass = acc_a[at, :]
                    for k in range(n5):
                        p = (R[at, (t * n5 + k) * LANES:(t * n5 + k + 1) * LANES] * w[k]) * a
                        mass = mass + p
                        low[k].append(p)
                    acc_a[at, :] = mass
            plan_low = jnp.concatenate(
                [jnp.concatenate(v, axis=0).astype(jnp.bfloat16) for v in low], axis=1
            )
            pulled = pulled + jnp.dot(plan_low, y[t * TILE5:(t + 1) * TILE5, :], preferred_element_type=f32)
        whole = pl.ds(base, ROWS5)
        mass_row = jnp.sum(acc_a[whole, :], axis=1, keepdims=True)
        part[whole, :] = mass_row * x[whole, :].astype(f32) - pulled
        to_cols(
            RS + b,
            lambda k: part.at[pl.ds(pl.multiple_of(base + k * share, share), share)],
            pr5.at[b, c],
        )
        pr5[b, c] = part[pl.ds(pl.multiple_of(base + c * share, share), share), :]
        return carry

    lax.fori_loop(0, rows // ROWS5, pass5, 0)

    for j in range(tiles):
        at = slice(j * SUB, (j + 1) * SUB)
        g_out[at, :] = (
            (2.0 * log_total + jnp.log2(rm[at, :]) - col2[at, :]) + jnp.log2(col4[at, :])
        ) * (1.0 / SCALE)

    def finish(b, carry):
        mine = pl.ds(pl.multiple_of(b * ROWS5 + c * share, share), share)
        arrived(RS + b, pr5.at[b, pl.ds(0, ncol - 1)])
        done[mine, :] = jnp.sum(pr5[b], axis=0)
        to_cols(AG + b, lambda k: done.at[mine], done.at[mine])
        return carry

    lax.fori_loop(0, rows // ROWS5, finish, 0)
    for b in range(rows // ROWS5):
        arrived(AG + b, done.at[pl.ds(0, ROWS5 - share)])
    grad_out[...] = done[...]

    for h in range(PARTS):
        left(Z1 + h, zr1.at[h, pl.ds(0, ncol - 1)])
        left(Z3 + h, zr3.at[h, pl.ds(0, ncol - 1)])
    left(A1, ra)
    left(A2, ta.at[pl.ds(0, chips - 1)])
    for j in range(half_tiles):
        mine = slice(j * SUB, (j + 1) * SUB)
        left(CORE2 + j, cs2.at[mine])
        left(CORE4 + j, cs4.at[mine])
        left(CHIP2 + j, ag2.at[pl.ds(0, chips - 1), mine])
        left(CHIP4 + j, ag4.at[pl.ds(0, chips - 1), mine])
    left(BACK2, col2.at[own_groups])
    left(BACK4, col4.at[own_groups])
    for b in range(rows // ROWS5):
        left(RS + b, pr5.at[b, pl.ds(0, ncol - 1)])
        left(AG + b, done.at[pl.ds(0, ROWS5 - share)])


def local(nrow, ncol, gen_points, ref_points, gen_mass, ref_mass):
    rows, width = gen_points.shape
    cols = ref_points.shape[0]
    row_blocks = rows // LANES
    groups = cols // LANES
    chunks = rows // CHUNK
    chips = nrow // 2
    vmem = pl.BlockSpec(memory_space=pltpu.VMEM)

    def buf(*shape):
        return pltpu.VMEM(shape, f32)

    def body(*refs):
        kernel(nrow, ncol, *refs)

    f, g, grad = pl.pallas_call(
        body,
        out_shape=(
            jax.ShapeDtypeStruct((row_blocks, LANES), f32),
            jax.ShapeDtypeStruct((groups, LANES), f32),
            jax.ShapeDtypeStruct((rows, width), f32),
        ),
        in_specs=[vmem] * 4,
        out_specs=(vmem, vmem, vmem),
        scratch_shapes=[
            buf(rows, cols), buf(chunks * SUB, cols), buf(SUB, cols), buf(SUB, cols), buf(groups, LANES),
            buf(rows, LANES), buf(rows, LANES), buf(rows, LANES), buf(row_blocks, LANES),
            buf(SUB, LANES), buf(SUB, LANES), buf(SUB, LANES), buf(chips, SUB, LANES),
            buf(PARTS, SUB, LANES), buf(PARTS, ncol, SUB, LANES),
            buf(PARTS, row_blocks // PARTS, LANES), buf(PARTS, ncol, row_blocks // PARTS, LANES),
            buf(groups, LANES), buf(groups, LANES), buf(groups // 2, LANES),
            buf(chips, groups // 2, LANES), buf(groups, LANES),
            buf(groups, LANES), buf(groups, LANES), buf(groups // 2, LANES),
            buf(chips, groups // 2, LANES), buf(groups, LANES),
            buf(SUB, width), buf(rows, width),
            buf(rows // ROWS5, ncol, ROWS5 // ncol, width), buf(rows, width),
            pltpu.SemaphoreType.DMA((32,)),
            pltpu.SemaphoreType.DMA((32,)),
        ],
        compiler_params=pltpu.CompilerParams(
            collective_id=0, has_side_effects=True, vmem_limit_bytes=56 * 2**20
        ),
        name="sinkhorn",
    )(gen_points, ref_points, gen_mass.reshape(row_blocks, LANES), ref_mass.reshape(groups, LANES))
    return f.reshape(rows), g.reshape(cols), grad


def solution(mesh):
    nrow, ncol = mesh.shape["row"], mesh.shape["col"]

    def run(*args):
        return local(nrow, ncol, *args)

    return jax.shard_map(
        run,
        mesh=mesh,
        in_specs=(P("row", None), P("col", None), P("row"), P("col")),
        out_specs=(P("row"), P("col"), P("row", None)),
        check_vma=False,
    )
```

```python
import math

import jax
import jax.numpy as jnp
from jax import lax
from jax.experimental import pallas as pl
from jax.experimental.pallas import tpu as pltpu
from jax.sharding import PartitionSpec as P

smoothing_epsilon = 0.05
SCALE = 1.0 / (smoothing_epsilon * math.log(2.0))
LANES = 128
SUB = 8
LOWEST = -3.0e38
f32 = jnp.float32
MESH = pl.DeviceIdType.MESH

CHUNK = 64
TILE0 = 2048
TILE1 = 4096
TILE2 = 4096
WIDE = 16
GROUPS3 = 16
GROUPS4 = 4
TILE5 = 2048
ROWS5 = 128
PARTS = 4
HALVES = 2


def scores(a, b):
    return lax.dot_general(a, b, (((1,), (1,)), ((), ())), preferred_element_type=f32)


def lane_cols(group):
    return pl.ds(pl.multiple_of(group * LANES, LANES), LANES)


def tile_rows(t):
    return pl.ds(pl.multiple_of(t * SUB, SUB), SUB)


def total(v):
    return jnp.sum(jnp.sum(v, axis=0, keepdims=True), axis=1, keepdims=True)


def log_sum(v):
    top = jnp.max(v, axis=0)
    return top + jnp.log2(jnp.sum(jnp.exp2(v - top[None]), axis=0))


def kernel(
    nrow, ncol, x, y_hbm, gm, rm, f_out, g_out, grad_out,
    y, R, MH, W, TOP, SUM, beta, acc_a, acc_b, lanes_u, row_f,
    sa, ra, ca, ta, zs1, zr1, zs3, zr3,
    cs2, cr2, gs2, ag2, col2, colw, cs4, cr4, gs4, ag4, col4,
    part, pr5, done, send_sem, recv_sem, load_sem,
):
    rows, width = x.shape
    cols = y.shape[0]
    loads = [
        pltpu.make_async_copy(
            y_hbm.at[pl.ds(t * TILE0, TILE0)], y.at[pl.ds(t * TILE0, TILE0)], load_sem.at[t]
        )
        for t in range(cols // TILE0)
    ]
    for load in loads:
        load.start()
    row_blocks = rows // LANES
    groups = cols // LANES
    tiles = groups // SUB
    half_tiles = tiles // 2
    half_groups = groups // 2
    chips = nrow // 2
    part_rows = rows // PARTS
    part_chunks = part_rows // CHUNK
    half_rows = rows // HALVES
    half_blocks = half_rows // LANES
    half_chunks = half_rows // CHUNK
    r = lax.axis_index("row")
    c = lax.axis_index("col")
    core = lax.rem(r, 2)
    chip = r // 2
    partner = 2 * chip + (1 - core)
    own = core * half_tiles
    other = (1 - core) * half_tiles

    def chip_peer(s):
        return lax.rem(r + 2 * s, nrow)

    def col_peer(s):
        return lax.rem(c + s, ncol)

    barrier = pltpu.get_barrier_semaphore()

    def greet_row(s, carry):
        pl.semaphore_signal(barrier, inc=1, device_id={"row": chip_peer(s)}, device_id_type=MESH)
        return carry

    def greet_col(s, carry):
        pl.semaphore_signal(barrier, inc=1, device_id={"col": col_peer(s)}, device_id_type=MESH)
        return carry

    pl.semaphore_signal(barrier, inc=1, device_id={"row": partner}, device_id_type=MESH)
    lax.fori_loop(1, chips, greet_row, 0)
    lax.fori_loop(1, ncol, greet_col, 0)

    def send(phase, device, source, target):
        pltpu.make_async_remote_copy(
            src_ref=source,
            dst_ref=target,
            send_sem=send_sem.at[phase],
            recv_sem=recv_sem.at[phase],
            device_id=device,
            device_id_type=MESH,
        ).start()

    def to_chips(phase, source, target):
        def one(s, carry):
            send(phase, {"row": chip_peer(s)}, source, target)
            return carry

        lax.fori_loop(1, chips, one, 0)

    def to_cols(phase, source, target):
        def one(s, carry):
            k = col_peer(s)
            send(phase, {"col": k}, source(k), target)
            return carry

        lax.fori_loop(1, ncol, one, 0)

    def arrived(phase, whole):
        pltpu.make_async_copy(whole, whole, recv_sem.at[phase]).wait()

    def left(phase, whole):
        pltpu.make_async_copy(whole, whole, send_sem.at[phase]).wait()

    Z1, Z3, CORE2, CHIP2, BACK2, CORE4, CHIP4, BACK4, A1, A2, RS, AG = (
        0, 4, 6, 10, 14, 15, 19, 23, 24, 25, 26, 34,
    )

    log_ref = jnp.log2(rm[...])
    beta[...] = log_ref
    zs1[...] = jnp.broadcast_to(total(rm[...])[None], zs1.shape)
    sa[...] = jnp.broadcast_to(total(gm[...]), sa.shape)
    acc_a[...] = jnp.full(acc_a.shape, LOWEST, f32)
    acc_b[...] = jnp.zeros(acc_b.shape, f32)
    TOP[...] = jnp.full(TOP.shape, LOWEST, f32)
    SUM[...] = jnp.zeros(SUM.shape, f32)

    def pass1(base, block, g0):
        rows_now = pl.ds(pl.multiple_of(base, part_rows), part_rows)
        tops, sums = acc_a.at[rows_now], acc_b.at[rows_now]
        for b in range(0, block.shape[1] // LANES, WIDE):
            bias = [beta[pl.ds(g0 + b + k, 1), :] for k in range(WIDE)]
            for i in range(0, part_rows, SUB):
                at = slice(i, i + SUB)
                e = [block[i:i + SUB, (b + k) * LANES:(b + k + 1) * LANES] * SCALE + bias[k] for k in range(WIDE)]
                old = tops[at, :]
                top = e[0]
                for v in e[1:]:
                    top = jnp.maximum(top, v)
                top = jnp.maximum(top, old)
                total_s = sums[at, :] * jnp.exp2(old - top)
                for v in e:
                    total_s = total_s + jnp.exp2(v - top)
                tops[at, :] = top
                sums[at, :] = total_s

    def report(h):
        o = pl.ds(pl.multiple_of(h * part_rows, part_rows), LANES)
        v = (acc_a[o, :] + jnp.log2(acc_b[o, :])).T
        top = jnp.max(v, axis=0, keepdims=True)
        zs1[h, 0:1, :] = top + jnp.log2(jnp.sum(jnp.exp2(v - top), axis=0, keepdims=True))

    def tell(h):
        to_cols(Z1 + h, lambda k: zs1.at[h], zr1.at[h, c])
        zr1[h, c] = zs1[h]

    n0 = TILE0 // LANES
    for t in range(cols // TILE0):
        loads[t].wait()
        points = y[t * TILE0:(t + 1) * TILE0, :]
        block = scores(x[0:part_rows, :], points)
        for k in range(n0):
            wide = points[k * LANES:(k + 1) * LANES, :].astype(f32)
            half = jnp.sum((wide * wide).T, axis=0, keepdims=True)
            g = t * n0 + k
            beta[g:g + 1, :] = beta[g:g + 1, :] - (0.5 * SCALE) * half
        pass1(0, block, t * n0)
    report(0)
    pl.semaphore_wait(barrier, chips + ncol - 1)
    tell(0)
    send(A1, {"row": partner}, sa, ra)

    n1 = TILE1 // LANES

    def pass1_part(h, carry):
        base = pl.multiple_of(h * part_rows, part_rows)

        def tile(t, carry):
            block = scores(x[pl.ds(base, part_rows), :], y[pl.ds(pl.multiple_of(t * TILE1, TILE1), TILE1), :])
            pass1(base, block, t * n1)
            return carry

        lax.fori_loop(0, cols // TILE1, tile, 0)
        report(h)
        tell(h)
        return carry

    lax.fori_loop(1, PARTS, pass1_part, 0)

    n2 = TILE2 // LANES
    t2 = n2 // SUB

    def spread(at, v):
        lanes_u[at, :] = jnp.broadcast_to(v, (LANES, LANES)).T

    def pass2(h, g0, last):
        base = pl.multiple_of(h * part_rows, part_rows)
        here = pl.ds(pl.multiple_of(g0 * LANES, TILE2), TILE2)
        block = scores(x[pl.ds(base, part_rows), :], y[here, :])
        powers = R.at[pl.ds(base, part_rows), here]
        u = lanes_u.at[pl.ds(base, part_rows)]
        marks = MH.at[pl.ds(pl.multiple_of(h * (part_chunks * SUB), SUB), part_chunks * SUB), here]
        top_now, sum_now = TOP.at[:, here], SUM.at[:, here]
        for b in range(0, n2, WIDE):
            cols_of = [slice(k * LANES, (k + 1) * LANES) for k in range(b, b + WIDE)]
            tops = [top_now[:, at] for at in cols_of]
            sums = [sum_now[:, at] for at in cols_of]
            bias = [beta[pl.ds(g0 + k, 1), :] for k in range(b, b + WIDE)]
            for j, at in enumerate(cols_of):
                top, s = tops[j], sums[j]
                for q in range(part_chunks):
                    span = range(q * CHUNK, (q + 1) * CHUNK, SUB)
                    e = [block[i:i + SUB, at] * SCALE + u[i:i + SUB, :] for i in span]
                    old = top
                    for v in e:
                        top = jnp.maximum(top, v)
                    s = s * jnp.exp2(old - top)
                    for i, v in zip(span, e):
                        z = jnp.exp2(v - top)
                        powers[i:i + SUB, at] = z
                        s = s + z
                    marks[q * SUB:(q + 1) * SUB, at] = top + bias[j]
                tops[j], sums[j] = top, s
            for j, at in enumerate(cols_of):
                if last:
                    best = jnp.max(tops[j], axis=0, keepdims=True)
                    s = jnp.sum(sums[j] * jnp.exp2(tops[j] - best), axis=0, keepdims=True)
                    cs2[pl.ds(g0 + b + j, 1), :] = best + jnp.log2(s) + bias[j]
                else:
                    top_now[:, at] = tops[j]
                    sum_now[:, at] = sums[j]

    def log_of_rows(h):
        arrived(Z1 + h, zr1.at[h, pl.ds(0, ncol - 1)])
        v = zr1[h]
        ref_total = jnp.sum(v, axis=0)[1:2, :]
        row_lse = log_sum(v)[0:1, :] - jnp.log2(ref_total)
        row_f[pl.ds(h, 1), :] = row_lse
        spread(pl.ds(pl.multiple_of(h * part_rows, part_rows), part_rows), jnp.log2(gm[pl.ds(h, 1), :]) - row_lse)
        return ref_total

    def pass2_part(h, carry):
        log_of_rows(h)

        def tile(t, carry):
            pass2(h, t * n2, False)
            return carry

        lax.fori_loop(0, groups // n2, tile, 0)
        return carry

    lax.fori_loop(0, PARTS - 1, pass2_part, 0)
    arrived(A1, ra)
    ca[...] = sa[...] + ra[...]
    to_chips(A2, ca, ta.at[chip])
    ta[chip] = ca[...]
    ref_total = log_of_rows(PARTS - 1)
    shares = jnp.log2(rm[...]) - jnp.log2(ref_total)

    def pass2_other(t, carry):
        g0 = other * SUB + t * n2
        pass2(PARTS - 1, g0, True)
        for j in range(t2):
            at = tile_rows(other + t * t2 + j)
            send(CORE2 + t * t2 + j, {"row": partner}, cs2.at[at], cr2.at[at])
        return carry

    def pass2_own(t, carry):
        g0 = own * SUB + t * n2
        pass2(PARTS - 1, g0, True)
        for j in range(t2):
            at = tile_rows(own + t * t2 + j)
            mine = tile_rows(t * t2 + j)
            arrived(CORE2 + t * t2 + j, cr2.at[at])
            a, b = cs2[at, :], cr2[at, :]
            top = jnp.maximum(a, b)
            both = top + jnp.log2(jnp.exp2(a - top) + jnp.exp2(b - top))
            gs2[mine, :] = both
            ag2[chip, mine, :] = both
            to_chips(CHIP2 + t * t2 + j, gs2.at[mine], ag2.at[chip, mine])
        return carry

    lax.fori_loop(0, half_groups // n2, pass2_other, 0)
    lax.fori_loop(0, half_groups // n2, pass2_own, 0)

    for j in range(half_tiles):
        mine = slice(j * SUB, (j + 1) * SUB)
        arrived(CHIP2 + j, ag2.at[pl.ds(0, chips - 1), mine])
        col2[tile_rows(own + j), :] = log_sum(ag2[:, mine, :])
    own_groups = pl.ds(pl.multiple_of(own * SUB, SUB), half_groups)
    other_groups = pl.ds(pl.multiple_of(other * SUB, SUB), half_groups)
    send(BACK2, {"row": partner}, col2.at[own_groups], col2.at[own_groups])
    colw[...] = -shares

    def weigh(half):
        colw[half, :] = col2[half, :] + colw[half, :]

    def pass3(first, h):
        def tile(t, carry):
            g0 = first * SUB + t * GROUPS3
            here = pl.ds(pl.multiple_of(g0 * LANES, GROUPS3 * LANES), GROUPS3 * LANES)
            powers, marks, weights = R.at[:, here], MH.at[:, here], W.at[:, here]
            cols_of = [slice(k * LANES, (k + 1) * LANES) for k in range(GROUPS3)]
            shift = [colw[pl.ds(g0 + k, 1), :] for k in range(GROUPS3)]
            for q in range(half_chunks):
                hq = (h * half_chunks + q) * SUB
                w = []
                for k, at in enumerate(cols_of):
                    v = jnp.exp2(marks[hq:hq + SUB, at] - shift[k])
                    weights[hq:hq + SUB, at] = v
                    w.append(v)
                for i in range(h * half_rows + q * CHUNK, h * half_rows + (q + 1) * CHUNK, SUB):
                    even = acc_a[i:i + SUB, :]
                    odd = jnp.zeros((SUB, LANES), f32)
                    for k, at in enumerate(cols_of):
                        v = powers[i:i + SUB, at] * w[k]
                        if k % 2:
                            odd = odd + v
                        else:
                            even = even + v
                    acc_a[i:i + SUB, :] = even + odd
            return carry

        lax.fori_loop(0, half_groups // GROUPS3, tile, 0)

    acc_a[...] = jnp.zeros(acc_a.shape, f32)
    weigh(own_groups)
    for h in range(HALVES):
        pass3(own, h)
    arrived(BACK2, col2.at[other_groups])
    weigh(other_groups)
    for h in range(HALVES):
        pass3(other, h)
        for k in range(half_blocks):
            o = (h * half_blocks + k) * LANES
            zs3[h, k:k + 1, :] = jnp.sum(acc_a[o:o + LANES, :].T, axis=0, keepdims=True)
        to_cols(Z3 + h, lambda k: zs3.at[h], zr3.at[h, c])
        zr3[h, c] = zs3[h]

    def pass4(h, g0):
        here = pl.ds(pl.multiple_of(g0 * LANES, GROUPS4 * LANES), GROUPS4 * LANES)
        powers, weights, partial = R.at[:, here], W.at[:, here], SUM.at[:, here]
        cols_of = [slice(k * LANES, (k + 1) * LANES) for k in range(GROUPS4)]
        sums = [partial[:, at] if h else jnp.zeros((SUB, LANES), f32) for at in cols_of]
        for q in range(half_chunks):
            hq = (h * half_chunks + q) * SUB
            inner = [jnp.zeros((SUB, LANES), f32) for _ in range(GROUPS4)]
            for i in range(h * half_rows + q * CHUNK, h * half_rows + (q + 1) * CHUNK, SUB):
                a = lanes_u[i:i + SUB, :]
                for k, at in enumerate(cols_of):
                    inner[k] = inner[k] + powers[i:i + SUB, at] * a
            for k, at in enumerate(cols_of):
                sums[k] = sums[k] + inner[k] * weights[hq:hq + SUB, at]
        for k, at in enumerate(cols_of):
            if h < HALVES - 1:
                partial[:, at] = sums[k]
            else:
                cs4[pl.ds(g0 + k, 1), :] = jnp.sum(sums[k], axis=0, keepdims=True)

    def scale_rows(h):
        arrived(Z3 + h, zr3.at[h, pl.ds(0, ncol - 1)])
        block = slice(h * half_blocks, (h + 1) * half_blocks)
        u = gm[block, :] / jnp.sum(zr3[h], axis=0)
        for k in range(half_blocks):
            o = (h * half_blocks + k) * LANES
            spread(slice(o, o + LANES), u[k:k + 1, :])
        row_f[block, :] = jnp.log2(u) - row_f[block, :]

    for h in range(HALVES - 1):
        scale_rows(h)

        def pass4_tile(t, carry, h=h):
            pass4(h, t * GROUPS4)
            return carry

        lax.fori_loop(0, groups // GROUPS4, pass4_tile, 0)
    scale_rows(HALVES - 1)

    def pass4_other(j, carry):
        for k in range(SUB // GROUPS4):
            pass4(HALVES - 1, (other + j) * SUB + k * GROUPS4)
        at = tile_rows(other + j)
        send(CORE4 + j, {"row": partner}, cs4.at[at], cr4.at[at])
        return carry

    def pass4_own(j, carry):
        for k in range(SUB // GROUPS4):
            pass4(HALVES - 1, (own + j) * SUB + k * GROUPS4)
        at = tile_rows(own + j)
        mine = tile_rows(j)
        arrived(CORE4 + j, cr4.at[at])
        both = cs4[at, :] + cr4[at, :]
        gs4[mine, :] = both
        ag4[chip, mine, :] = both
        to_chips(CHIP4 + j, gs4.at[mine], ag4.at[chip, mine])
        return carry

    lax.fori_loop(0, half_tiles, pass4_other, 0)
    lax.fori_loop(0, half_tiles, pass4_own, 0)

    arrived(A2, ta.at[pl.ds(0, chips - 1)])
    log_total = jnp.log2(jnp.sum(ta[...], axis=0)[0:1, :])
    for k in range(row_blocks):
        wide = x[k * LANES:(k + 1) * LANES, :].astype(f32)
        half = 0.5 * jnp.sum((wide * wide).T, axis=0, keepdims=True)
        f_out[k:k + 1, :] = half + (row_f[k:k + 1, :] - log_total) * (1.0 / SCALE)
    lanes_u[...] = lanes_u[...] * float(rows * nrow)
    acc_a[...] = jnp.zeros(acc_a.shape, f32)

    for j in range(half_tiles):
        mine = slice(j * SUB, (j + 1) * SUB)
        at = tile_rows(own + j)
        arrived(CHIP4 + j, ag4.at[pl.ds(0, chips - 1), mine])
        col4[at, :] = rm[at, :] / (ref_total * jnp.sum(ag4[:, mine, :], axis=0))
    send(BACK4, {"row": partner}, col4.at[own_groups], col4.at[own_groups])
    arrived(BACK4, col4.at[other_groups])

    n5 = TILE5 // LANES
    share = ROWS5 // ncol

    def pass5(b, carry):
        base = pl.multiple_of(b * ROWS5, ROWS5)
        whole = pl.ds(base, ROWS5)
        powers, u, masses = R.at[whole], lanes_u.at[whole], acc_a.at[whole]
        chunks_here = ROWS5 // CHUNK
        weights = W.at[pl.ds(pl.multiple_of(b * (chunks_here * SUB), SUB), chunks_here * SUB)]
        pulled = jnp.zeros((ROWS5, width), f32)
        for t in range(cols // TILE5):
            low = [[] for _ in range(n5)]
            for q in range(ROWS5 // CHUNK):
                hq = slice(q * SUB, (q + 1) * SUB)
                w = [weights[hq, (t * n5 + k) * LANES:(t * n5 + k + 1) * LANES] * col4[t * n5 + k:t * n5 + k + 1, :]
                     for k in range(n5)]
                for i in range(q * CHUNK, (q + 1) * CHUNK, SUB):
                    at = slice(i, i + SUB)
                    a = u[at, :]
                    mass = masses[at, :]
                    for k in range(n5):
                        p = (powers[at, (t * n5 + k) * LANES:(t * n5 + k + 1) * LANES] * w[k]) * a
                        mass = mass + p
                        low[k].append(p)
                    masses[at, :] = mass
            plan_low = jnp.concatenate(
                [jnp.concatenate(v, axis=0).astype(jnp.bfloat16) for v in low], axis=1
            )
            pulled = pulled + jnp.dot(plan_low, y[t * TILE5:(t + 1) * TILE5, :], preferred_element_type=f32)
        mass_row = jnp.sum(masses[...], axis=1, keepdims=True)
        part[whole, :] = mass_row * x[whole, :].astype(f32) - pulled
        to_cols(
            RS + b,
            lambda k: part.at[pl.ds(pl.multiple_of(base + k * share, share), share)],
            pr5.at[b, c],
        )
        pr5[b, c] = part[pl.ds(pl.multiple_of(base + c * share, share), share), :]
        return carry

    lax.fori_loop(0, rows // ROWS5, pass5, 0)

    for j in range(tiles):
        at = slice(j * SUB, (j + 1) * SUB)
        g_out[at, :] = (
            (2.0 * log_total + jnp.log2(rm[at, :]) - col2[at, :]) + jnp.log2(col4[at, :])
        ) * (1.0 / SCALE)

    def finish(b, carry):
        mine = pl.ds(pl.multiple_of(b * ROWS5 + c * share, share), share)
        arrived(RS + b, pr5.at[b, pl.ds(0, ncol - 1)])
        done[mine, :] = jnp.sum(pr5[b], axis=0)
        to_cols(AG + b, lambda k: done.at[mine], done.at[mine])
        return carry

    lax.fori_loop(0, rows // ROWS5, finish, 0)
    for b in range(rows // ROWS5):
        arrived(AG + b, done.at[pl.ds(0, ROWS5 - share)])
    grad_out[...] = done[...]

    for h in range(PARTS):
        left(Z1 + h, zr1.at[h, pl.ds(0, ncol - 1)])
    for h in range(HALVES):
        left(Z3 + h, zr3.at[h, pl.ds(0, ncol - 1)])
    left(A1, ra)
    left(A2, ta.at[pl.ds(0, chips - 1)])
    for j in range(half_tiles):
        mine = slice(j * SUB, (j + 1) * SUB)
        left(CORE2 + j, cs2.at[mine])
        left(CORE4 + j, cs4.at[mine])
        left(CHIP2 + j, ag2.at[pl.ds(0, chips - 1), mine])
        left(CHIP4 + j, ag4.at[pl.ds(0, chips - 1), mine])
    left(BACK2, col2.at[own_groups])
    left(BACK4, col4.at[own_groups])
    for b in range(rows // ROWS5):
        left(RS + b, pr5.at[b, pl.ds(0, ncol - 1)])
        left(AG + b, done.at[pl.ds(0, ROWS5 - share)])


def move(f, g, grad, f_out, g_out, grad_out):
    f_out[...] = f[...]
    g_out[...] = g[...]
    grad_out[...] = grad[...]


def hand_on(*arrays):
    vmem = pl.BlockSpec(memory_space=pltpu.VMEM)
    return pl.pallas_call(
        move,
        out_shape=tuple(jax.ShapeDtypeStruct(a.shape, a.dtype) for a in arrays),
        in_specs=[vmem] * 3,
        out_specs=(vmem,) * 3,
        name="hand_on",
    )(*arrays)


def local(nrow, ncol, gen_points, ref_points, gen_mass, ref_mass):
    rows, width = gen_points.shape
    cols = ref_points.shape[0]
    row_blocks = rows // LANES
    groups = cols // LANES
    chunks = rows // CHUNK
    chips = nrow // 2
    vmem = pl.BlockSpec(memory_space=pltpu.VMEM)
    anywhere = pl.BlockSpec(memory_space=pl.ANY)

    def buf(*shape):
        return pltpu.VMEM(shape, f32)

    def body(*refs):
        kernel(nrow, ncol, *refs)

    f, g, grad = pl.pallas_call(
        body,
        out_shape=(
            jax.ShapeDtypeStruct((row_blocks, LANES), f32),
            jax.ShapeDtypeStruct((groups, LANES), f32),
            jax.ShapeDtypeStruct((rows, width), f32),
        ),
        in_specs=[vmem, anywhere, vmem, vmem],
        out_specs=(vmem, vmem, vmem),
        scratch_shapes=[
            pltpu.VMEM((cols, width), ref_points.dtype), buf(rows, cols), buf(chunks * SUB, cols), buf(chunks * SUB, cols), buf(SUB, cols), buf(SUB, cols), buf(groups, LANES),
            buf(rows, LANES), buf(rows, LANES), buf(rows, LANES), buf(row_blocks, LANES),
            buf(SUB, LANES), buf(SUB, LANES), buf(SUB, LANES), buf(chips, SUB, LANES),
            buf(PARTS, SUB, LANES), buf(PARTS, ncol, SUB, LANES),
            buf(HALVES, row_blocks // HALVES, LANES), buf(HALVES, ncol, row_blocks // HALVES, LANES),
            buf(groups, LANES), buf(groups, LANES), buf(groups // 2, LANES),
            buf(chips, groups // 2, LANES), buf(groups, LANES), buf(groups, LANES),
            buf(groups, LANES), buf(groups, LANES), buf(groups // 2, LANES),
            buf(chips, groups // 2, LANES), buf(groups, LANES),
            buf(rows, width),
            buf(rows // ROWS5, ncol, ROWS5 // ncol, width), buf(rows, width),
            pltpu.SemaphoreType.DMA((42,)),
            pltpu.SemaphoreType.DMA((42,)),
            pltpu.SemaphoreType.DMA((cols // TILE0,)),
        ],
        compiler_params=pltpu.CompilerParams(
            collective_id=0, has_side_effects=True, vmem_limit_bytes=56 * 2**20
        ),
        name="sinkhorn",
    )(gen_points, ref_points, gen_mass.reshape(row_blocks, LANES), ref_mass.reshape(groups, LANES))
    f, g, grad = hand_on(f, g, grad)
    return f.reshape(rows), g.reshape(cols), grad


def solution(mesh):
    nrow, ncol = mesh.shape["row"], mesh.shape["col"]

    def run(*args):
        return local(nrow, ncol, *args)

    return jax.shard_map(
        run,
        mesh=mesh,
        in_specs=(P("row", None), P("col", None), P("row"), P("col")),
        out_specs=(P("row"), P("col"), P("row", None)),
        check_vma=False,
    )
```

```python
import math

import jax
import jax.numpy as jnp
from jax import lax
from jax.experimental import pallas as pl
from jax.experimental.pallas import tpu as pltpu
from jax.sharding import PartitionSpec as P

smoothing_epsilon = 0.05
SCALE = 1.0 / (smoothing_epsilon * math.log(2.0))
LANES = 128
SUB = 8
LOWEST = -3.0e38
f32 = jnp.float32
MESH = pl.DeviceIdType.MESH

CHUNK = 64
TILE0 = 2048
TILE1 = 4096
TILE2 = 4096
WIDE = 16
GROUPS3 = 16
GROUPS4 = 4
TILE5 = 2048
ROWS5 = 128
PARTS = 4
HALVES = 2


def scores(a, b):
    return lax.dot_general(a, b, (((1,), (1,)), ((), ())), preferred_element_type=f32)


def lane_cols(group):
    return pl.ds(pl.multiple_of(group * LANES, LANES), LANES)


def tile_rows(t):
    return pl.ds(pl.multiple_of(t * SUB, SUB), SUB)


def total(v):
    return jnp.sum(jnp.sum(v, axis=0, keepdims=True), axis=1, keepdims=True)


def log_sum(v):
    top = jnp.max(v, axis=0)
    return top + jnp.log2(jnp.sum(jnp.exp2(v - top[None]), axis=0))


def kernel(
    nrow, ncol, x, y_hbm, gm, rm, f_out, g_out, grad_out,
    y, R, MH, W, TOP, SUM, beta, acc_a, acc_b, lanes_u, row_f,
    sa, ra, ca, ta, zs1, zr1, zs3, zr3,
    cs2, cr2, gs2, ag2, col2, colw, cs4, cr4, gs4, ag4, col4,
    part, pr5, done, send_sem, recv_sem, load_sem,
):
    rows, width = x.shape
    cols = y.shape[0]
    loads = [
        pltpu.make_async_copy(
            y_hbm.at[pl.ds(t * TILE0, TILE0)], y.at[pl.ds(t * TILE0, TILE0)], load_sem.at[t]
        )
        for t in range(cols // TILE0)
    ]
    for load in loads:
        load.start()
    row_blocks = rows // LANES
    groups = cols // LANES
    tiles = groups // SUB
    half_tiles = tiles // 2
    half_groups = groups // 2
    chips = nrow // 2
    part_rows = rows // PARTS
    part_chunks = part_rows // CHUNK
    half_rows = rows // HALVES
    half_blocks = half_rows // LANES
    half_chunks = half_rows // CHUNK
    r = lax.axis_index("row")
    c = lax.axis_index("col")
    core = lax.rem(r, 2)
    chip = r // 2
    partner = 2 * chip + (1 - core)
    own = core * half_tiles
    other = (1 - core) * half_tiles

    def chip_peer(s):
        return lax.rem(r + 2 * s, nrow)

    def col_peer(s):
        return lax.rem(c + s, ncol)

    col_order = sorted(range(1, ncol), key=lambda s: -min(s, ncol - s))
    side = math.isqrt(chips)
    chip_order = sorted(
        range(1, chips),
        key=lambda s: -(min(s // side, side - s // side) + min(s % side, side - s % side)),
    )

    barrier = pltpu.get_barrier_semaphore()

    def greet_row(s, carry):
        pl.semaphore_signal(barrier, inc=1, device_id={"row": chip_peer(s)}, device_id_type=MESH)
        return carry

    def greet_col(s, carry):
        pl.semaphore_signal(barrier, inc=1, device_id={"col": col_peer(s)}, device_id_type=MESH)
        return carry

    pl.semaphore_signal(barrier, inc=1, device_id={"row": partner}, device_id_type=MESH)
    lax.fori_loop(1, chips, greet_row, 0)
    lax.fori_loop(1, ncol, greet_col, 0)

    def send(phase, device, source, target):
        pltpu.make_async_remote_copy(
            src_ref=source,
            dst_ref=target,
            send_sem=send_sem.at[phase],
            recv_sem=recv_sem.at[phase],
            device_id=device,
            device_id_type=MESH,
        ).start()

    def to_chips(phase, source, target):
        def one(s, carry):
            send(phase, {"row": chip_peer(s)}, source, target)
            return carry

        for s in chip_order:
            one(s, 0)

    def to_cols(phase, source, target):
        def one(s, carry):
            k = col_peer(s)
            send(phase, {"col": k}, source(k), target)
            return carry

        for s in col_order:
            one(s, 0)

    def arrived(phase, whole):
        pltpu.make_async_copy(whole, whole, recv_sem.at[phase]).wait()

    def left(phase, whole):
        pltpu.make_async_copy(whole, whole, send_sem.at[phase]).wait()

    Z1, Z3, CORE2, CHIP2, BACK2, CORE4, CHIP4, BACK4, A1, A2, RS, AG = (
        0, 4, 6, 10, 14, 15, 19, 23, 24, 25, 26, 34,
    )

    log_ref = jnp.log2(rm[...])
    beta[...] = log_ref
    zs1[...] = jnp.broadcast_to(total(rm[...])[None], zs1.shape)
    sa[...] = jnp.broadcast_to(total(gm[...]), sa.shape)
    acc_a[...] = jnp.full(acc_a.shape, LOWEST, f32)
    acc_b[...] = jnp.zeros(acc_b.shape, f32)
    TOP[...] = jnp.full(TOP.shape, LOWEST, f32)
    SUM[...] = jnp.zeros(SUM.shape, f32)

    def pass1(base, block, g0):
        rows_now = pl.ds(pl.multiple_of(base, part_rows), part_rows)
        tops, sums = acc_a.at[rows_now], acc_b.at[rows_now]
        for b in range(0, block.shape[1] // LANES, WIDE):
            bias = [beta[pl.ds(g0 + b + k, 1), :] for k in range(WIDE)]
            for i in range(0, part_rows, SUB):
                at = slice(i, i + SUB)
                e = [block[i:i + SUB, (b + k) * LANES:(b + k + 1) * LANES] * SCALE + bias[k] for k in range(WIDE)]
                old = tops[at, :]
                top = e[0]
                for v in e[1:]:
                    top = jnp.maximum(top, v)
                top = jnp.maximum(top, old)
                total_s = sums[at, :] * jnp.exp2(old - top)
                for v in e:
                    total_s = total_s + jnp.exp2(v - top)
                tops[at, :] = top
                sums[at, :] = total_s

    def report(h):
        o = pl.ds(pl.multiple_of(h * part_rows, part_rows), LANES)
        v = (acc_a[o, :] + jnp.log2(acc_b[o, :])).T
        top = jnp.max(v, axis=0, keepdims=True)
        zs1[h, 0:1, :] = top + jnp.log2(jnp.sum(jnp.exp2(v - top), axis=0, keepdims=True))

    def tell(h):
        to_cols(Z1 + h, lambda k: zs1.at[h], zr1.at[h, c])
        zr1[h, c] = zs1[h]

    n0 = TILE0 // LANES
    for t in range(cols // TILE0):
        loads[t].wait()
        points = y[t * TILE0:(t + 1) * TILE0, :]
        block = scores(x[0:part_rows, :], points)
        for k in range(n0):
            wide = points[k * LANES:(k + 1) * LANES, :].astype(f32)
            half = jnp.sum((wide * wide).T, axis=0, keepdims=True)
            g = t * n0 + k
            beta[g:g + 1, :] = beta[g:g + 1, :] - (0.5 * SCALE) * half
        pass1(0, block, t * n0)
    report(0)
    pl.semaphore_wait(barrier, chips + ncol - 1)
    tell(0)
    send(A1, {"row": partner}, sa, ra)

    n1 = TILE1 // LANES

    def pass1_part(h, carry):
        base = pl.multiple_of(h * part_rows, part_rows)

        def tile(t, carry):
            block = scores(x[pl.ds(base, part_rows), :], y[pl.ds(pl.multiple_of(t * TILE1, TILE1), TILE1), :])
            pass1(base, block, t * n1)
            return carry

        lax.fori_loop(0, cols // TILE1, tile, 0, unroll=True)
        report(h)
        tell(h)
        return carry

    lax.fori_loop(1, PARTS, pass1_part, 0)

    n2 = TILE2 // LANES
    t2 = n2 // SUB

    def spread(at, v):
        lanes_u[at, :] = jnp.broadcast_to(v, (LANES, LANES)).T

    def pass2(h, g0, last):
        base = pl.multiple_of(h * part_rows, part_rows)
        here = pl.ds(pl.multiple_of(g0 * LANES, TILE2), TILE2)
        block = scores(x[pl.ds(base, part_rows), :], y[here, :])
        powers = R.at[pl.ds(base, part_rows), here]
        u = lanes_u.at[pl.ds(base, part_rows)]
        marks = MH.at[pl.ds(pl.multiple_of(h * (part_chunks * SUB), SUB), part_chunks * SUB), here]
        top_now, sum_now = TOP.at[:, here], SUM.at[:, here]
        for b in range(0, n2, WIDE):
            cols_of = [slice(k * LANES, (k + 1) * LANES) for k in range(b, b + WIDE)]
            tops = [top_now[:, at] for at in cols_of]
            sums = [sum_now[:, at] for at in cols_of]
            bias = [beta[pl.ds(g0 + k, 1), :] for k in range(b, b + WIDE)]
            for j, at in enumerate(cols_of):
                top, s = tops[j], sums[j]
                for q in range(part_chunks):
                    span = range(q * CHUNK, (q + 1) * CHUNK, SUB)
                    e = [block[i:i + SUB, at] * SCALE + u[i:i + SUB, :] for i in span]
                    old = top
                    for v in e:
                        top = jnp.maximum(top, v)
                    s = s * jnp.exp2(old - top)
                    for i, v in zip(span, e):
                        z = jnp.exp2(v - top)
                        powers[i:i + SUB, at] = z
                        s = s + z
                    marks[q * SUB:(q + 1) * SUB, at] = top + bias[j]
                tops[j], sums[j] = top, s
            for j, at in enumerate(cols_of):
                if last:
                    best = jnp.max(tops[j], axis=0, keepdims=True)
                    s = jnp.sum(sums[j] * jnp.exp2(tops[j] - best), axis=0, keepdims=True)
                    cs2[pl.ds(g0 + b + j, 1), :] = best + jnp.log2(s) + bias[j]
                else:
                    top_now[:, at] = tops[j]
                    sum_now[:, at] = sums[j]

    def log_of_rows(h):
        arrived(Z1 + h, zr1.at[h, pl.ds(0, ncol - 1)])
        v = zr1[h]
        ref_total = jnp.sum(v, axis=0)[1:2, :]
        row_lse = log_sum(v)[0:1, :] - jnp.log2(ref_total)
        row_f[pl.ds(h, 1), :] = row_lse
        spread(pl.ds(pl.multiple_of(h * part_rows, part_rows), part_rows), jnp.log2(gm[pl.ds(h, 1), :]) - row_lse)
        return ref_total

    def pass2_part(h, carry):
        log_of_rows(h)

        def tile(t, carry):
            pass2(h, t * n2, False)
            return carry

        lax.fori_loop(0, groups // n2, tile, 0, unroll=True)
        return carry

    lax.fori_loop(0, PARTS - 1, pass2_part, 0)
    arrived(A1, ra)
    ca[...] = sa[...] + ra[...]
    to_chips(A2, ca, ta.at[chip])
    ta[chip] = ca[...]
    ref_total = log_of_rows(PARTS - 1)
    shares = jnp.log2(rm[...]) - jnp.log2(ref_total)

    def pass2_other(t, carry):
        g0 = other * SUB + t * n2
        pass2(PARTS - 1, g0, True)
        for j in range(t2):
            at = tile_rows(other + t * t2 + j)
            send(CORE2 + t * t2 + j, {"row": partner}, cs2.at[at], cr2.at[at])
        return carry

    def pass2_own(t, carry):
        g0 = own * SUB + t * n2
        pass2(PARTS - 1, g0, True)
        for j in range(t2):
            at = tile_rows(own + t * t2 + j)
            mine = tile_rows(t * t2 + j)
            arrived(CORE2 + t * t2 + j, cr2.at[at])
            a, b = cs2[at, :], cr2[at, :]
            top = jnp.maximum(a, b)
            both = top + jnp.log2(jnp.exp2(a - top) + jnp.exp2(b - top))
            gs2[mine, :] = both
            ag2[chip, mine, :] = both
            to_chips(CHIP2 + t * t2 + j, gs2.at[mine], ag2.at[chip, mine])
        return carry

    lax.fori_loop(0, half_groups // n2, pass2_other, 0)
    lax.fori_loop(0, half_groups // n2, pass2_own, 0)

    for j in range(half_tiles):
        mine = slice(j * SUB, (j + 1) * SUB)
        arrived(CHIP2 + j, ag2.at[pl.ds(0, chips - 1), mine])
        col2[tile_rows(own + j), :] = log_sum(ag2[:, mine, :])
    own_groups = pl.ds(pl.multiple_of(own * SUB, SUB), half_groups)
    other_groups = pl.ds(pl.multiple_of(other * SUB, SUB), half_groups)
    send(BACK2, {"row": partner}, col2.at[own_groups], col2.at[own_groups])
    colw[...] = -shares

    def weigh(half):
        colw[half, :] = col2[half, :] + colw[half, :]

    def pass3(first, h):
        def tile(t, carry):
            g0 = first * SUB + t * GROUPS3
            here = pl.ds(pl.multiple_of(g0 * LANES, GROUPS3 * LANES), GROUPS3 * LANES)
            powers, marks, weights = R.at[:, here], MH.at[:, here], W.at[:, here]
            cols_of = [slice(k * LANES, (k + 1) * LANES) for k in range(GROUPS3)]
            shift = [colw[pl.ds(g0 + k, 1), :] for k in range(GROUPS3)]
            for q in range(half_chunks):
                hq = (h * half_chunks + q) * SUB
                w = []
                for k, at in enumerate(cols_of):
                    v = jnp.exp2(marks[hq:hq + SUB, at] - shift[k])
                    weights[hq:hq + SUB, at] = v
                    w.append(v)
                for i in range(h * half_rows + q * CHUNK, h * half_rows + (q + 1) * CHUNK, SUB):
                    even = acc_a[i:i + SUB, :]
                    odd = jnp.zeros((SUB, LANES), f32)
                    for k, at in enumerate(cols_of):
                        v = powers[i:i + SUB, at] * w[k]
                        if k % 2:
                            odd = odd + v
                        else:
                            even = even + v
                    acc_a[i:i + SUB, :] = even + odd
            return carry

        lax.fori_loop(0, half_groups // GROUPS3, tile, 0)

    acc_a[...] = jnp.zeros(acc_a.shape, f32)
    weigh(own_groups)
    for h in range(HALVES):
        pass3(own, h)
    arrived(BACK2, col2.at[other_groups])
    weigh(other_groups)
    for h in range(HALVES):
        pass3(other, h)
        for k in range(half_blocks):
            o = (h * half_blocks + k) * LANES
            zs3[h, k:k + 1, :] = jnp.sum(acc_a[o:o + LANES, :].T, axis=0, keepdims=True)
        to_cols(Z3 + h, lambda k: zs3.at[h], zr3.at[h, c])
        zr3[h, c] = zs3[h]

    def pass4(h, g0):
        here = pl.ds(pl.multiple_of(g0 * LANES, GROUPS4 * LANES), GROUPS4 * LANES)
        powers, weights, partial = R.at[:, here], W.at[:, here], SUM.at[:, here]
        cols_of = [slice(k * LANES, (k + 1) * LANES) for k in range(GROUPS4)]
        sums = [partial[:, at] if h else jnp.zeros((SUB, LANES), f32) for at in cols_of]
        for q in range(half_chunks):
            hq = (h * half_chunks + q) * SUB
            inner = [jnp.zeros((SUB, LANES), f32) for _ in range(GROUPS4)]
            for i in range(h * half_rows + q * CHUNK, h * half_rows + (q + 1) * CHUNK, SUB):
                a = lanes_u[i:i + SUB, :]
                for k, at in enumerate(cols_of):
                    inner[k] = inner[k] + powers[i:i + SUB, at] * a
            for k, at in enumerate(cols_of):
                sums[k] = sums[k] + inner[k] * weights[hq:hq + SUB, at]
        for k, at in enumerate(cols_of):
            if h < HALVES - 1:
                partial[:, at] = sums[k]
            else:
                cs4[pl.ds(g0 + k, 1), :] = jnp.sum(sums[k], axis=0, keepdims=True)

    def scale_rows(h):
        arrived(Z3 + h, zr3.at[h, pl.ds(0, ncol - 1)])
        block = slice(h * half_blocks, (h + 1) * half_blocks)
        u = gm[block, :] / jnp.sum(zr3[h], axis=0)
        for k in range(half_blocks):
            o = (h * half_blocks + k) * LANES
            spread(slice(o, o + LANES), u[k:k + 1, :])
        row_f[block, :] = jnp.log2(u) - row_f[block, :]

    for h in range(HALVES - 1):
        scale_rows(h)

        def pass4_tile(t, carry, h=h):
            pass4(h, t * GROUPS4)
            return carry

        lax.fori_loop(0, groups // GROUPS4, pass4_tile, 0)
    scale_rows(HALVES - 1)

    def pass4_other(j, carry):
        for k in range(SUB // GROUPS4):
            pass4(HALVES - 1, (other + j) * SUB + k * GROUPS4)
        at = tile_rows(other + j)
        send(CORE4 + j, {"row": partner}, cs4.at[at], cr4.at[at])
        return carry

    def pass4_own(j, carry):
        for k in range(SUB // GROUPS4):
            pass4(HALVES - 1, (own + j) * SUB + k * GROUPS4)
        at = tile_rows(own + j)
        mine = tile_rows(j)
        arrived(CORE4 + j, cr4.at[at])
        both = cs4[at, :] + cr4[at, :]
        gs4[mine, :] = both
        ag4[chip, mine, :] = both
        to_chips(CHIP4 + j, gs4.at[mine], ag4.at[chip, mine])
        return carry

    lax.fori_loop(0, half_tiles, pass4_other, 0)
    lax.fori_loop(0, half_tiles, pass4_own, 0)

    arrived(A2, ta.at[pl.ds(0, chips - 1)])
    log_total = jnp.log2(jnp.sum(ta[...], axis=0)[0:1, :])
    for k in range(row_blocks):
        wide = x[k * LANES:(k + 1) * LANES, :].astype(f32)
        half = 0.5 * jnp.sum((wide * wide).T, axis=0, keepdims=True)
        f_out[k:k + 1, :] = half + (row_f[k:k + 1, :] - log_total) * (1.0 / SCALE)
    lanes_u[...] = lanes_u[...] * float(rows * nrow)
    acc_a[...] = jnp.zeros(acc_a.shape, f32)

    for j in range(half_tiles):
        mine = slice(j * SUB, (j + 1) * SUB)
        at = tile_rows(own + j)
        arrived(CHIP4 + j, ag4.at[pl.ds(0, chips - 1), mine])
        col4[at, :] = rm[at, :] / (ref_total * jnp.sum(ag4[:, mine, :], axis=0))
    send(BACK4, {"row": partner}, col4.at[own_groups], col4.at[own_groups])
    arrived(BACK4, col4.at[other_groups])

    n5 = TILE5 // LANES
    share = ROWS5 // ncol

    def pass5(b, carry):
        base = pl.multiple_of(b * ROWS5, ROWS5)
        whole = pl.ds(base, ROWS5)
        powers, u, masses = R.at[whole], lanes_u.at[whole], acc_a.at[whole]
        chunks_here = ROWS5 // CHUNK
        weights = W.at[pl.ds(pl.multiple_of(b * (chunks_here * SUB), SUB), chunks_here * SUB)]
        pulled = jnp.zeros((ROWS5, width), f32)
        for t in range(cols // TILE5):
            low = [[] for _ in range(n5)]
            for q in range(ROWS5 // CHUNK):
                hq = slice(q * SUB, (q + 1) * SUB)
                w = [weights[hq, (t * n5 + k) * LANES:(t * n5 + k + 1) * LANES] * col4[t * n5 + k:t * n5 + k + 1, :]
                     for k in range(n5)]
                for i in range(q * CHUNK, (q + 1) * CHUNK, SUB):
                    at = slice(i, i + SUB)
                    a = u[at, :]
                    mass = masses[at, :]
                    for k in range(n5):
                        p = (powers[at, (t * n5 + k) * LANES:(t * n5 + k + 1) * LANES] * w[k]) * a
                        mass = mass + p
                        low[k].append(p)
                    masses[at, :] = mass
            plan_low = jnp.concatenate(
                [jnp.concatenate(v, axis=0).astype(jnp.bfloat16) for v in low], axis=1
            )
            pulled = pulled + jnp.dot(plan_low, y[t * TILE5:(t + 1) * TILE5, :], preferred_element_type=f32)
        mass_row = jnp.sum(masses[...], axis=1, keepdims=True)
        part[whole, :] = mass_row * x[whole, :].astype(f32) - pulled
        to_cols(
            RS + b,
            lambda k: part.at[pl.ds(pl.multiple_of(base + k * share, share), share)],
            pr5.at[b, c],
        )
        pr5[b, c] = part[pl.ds(pl.multiple_of(base + c * share, share), share), :]
        return carry

    lax.fori_loop(0, rows // ROWS5, pass5, 0)

    for j in range(tiles):
        at = slice(j * SUB, (j + 1) * SUB)
        g_out[at, :] = (
            (2.0 * log_total + jnp.log2(rm[at, :]) - col2[at, :]) + jnp.log2(col4[at, :])
        ) * (1.0 / SCALE)

    def finish(b, carry):
        mine = pl.ds(pl.multiple_of(b * ROWS5 + c * share, share), share)
        arrived(RS + b, pr5.at[b, pl.ds(0, ncol - 1)])
        done[mine, :] = jnp.sum(pr5[b], axis=0)
        to_cols(AG + b, lambda k: done.at[mine], done.at[mine])
        return carry

    lax.fori_loop(0, rows // ROWS5, finish, 0)
    for b in range(rows // ROWS5):
        arrived(AG + b, done.at[pl.ds(0, ROWS5 - share)])
    grad_out[...] = done[...]

    for h in range(PARTS):
        left(Z1 + h, zr1.at[h, pl.ds(0, ncol - 1)])
    for h in range(HALVES):
        left(Z3 + h, zr3.at[h, pl.ds(0, ncol - 1)])
    left(A1, ra)
    left(A2, ta.at[pl.ds(0, chips - 1)])
    for j in range(half_tiles):
        mine = slice(j * SUB, (j + 1) * SUB)
        left(CORE2 + j, cs2.at[mine])
        left(CORE4 + j, cs4.at[mine])
        left(CHIP2 + j, ag2.at[pl.ds(0, chips - 1), mine])
        left(CHIP4 + j, ag4.at[pl.ds(0, chips - 1), mine])
    left(BACK2, col2.at[own_groups])
    left(BACK4, col4.at[own_groups])
    for b in range(rows // ROWS5):
        left(RS + b, pr5.at[b, pl.ds(0, ncol - 1)])
        left(AG + b, done.at[pl.ds(0, ROWS5 - share)])


def move(f, g, grad, f_out, g_out, grad_out):
    f_out[...] = f[...]
    g_out[...] = g[...]
    grad_out[...] = grad[...]


def hand_on(*arrays):
    vmem = pl.BlockSpec(memory_space=pltpu.VMEM)
    return pl.pallas_call(
        move,
        out_shape=tuple(jax.ShapeDtypeStruct(a.shape, a.dtype) for a in arrays),
        in_specs=[vmem] * 3,
        out_specs=(vmem,) * 3,
        name="hand_on",
    )(*arrays)


def local(nrow, ncol, gen_points, ref_points, gen_mass, ref_mass):
    rows, width = gen_points.shape
    cols = ref_points.shape[0]
    row_blocks = rows // LANES
    groups = cols // LANES
    chunks = rows // CHUNK
    chips = nrow // 2
    vmem = pl.BlockSpec(memory_space=pltpu.VMEM)
    anywhere = pl.BlockSpec(memory_space=pl.ANY)

    def buf(*shape):
        return pltpu.VMEM(shape, f32)

    def body(*refs):
        kernel(nrow, ncol, *refs)

    f, g, grad = pl.pallas_call(
        body,
        out_shape=(
            jax.ShapeDtypeStruct((row_blocks, LANES), f32),
            jax.ShapeDtypeStruct((groups, LANES), f32),
            jax.ShapeDtypeStruct((rows, width), f32),
        ),
        in_specs=[vmem, anywhere, vmem, vmem],
        out_specs=(vmem, vmem, vmem),
        scratch_shapes=[
            pltpu.VMEM((cols, width), ref_points.dtype), buf(rows, cols), buf(chunks * SUB, cols), buf(chunks * SUB, cols), buf(SUB, cols), buf(SUB, cols), buf(groups, LANES),
            buf(rows, LANES), buf(rows, LANES), buf(rows, LANES), buf(row_blocks, LANES),
            buf(SUB, LANES), buf(SUB, LANES), buf(SUB, LANES), buf(chips, SUB, LANES),
            buf(PARTS, SUB, LANES), buf(PARTS, ncol, SUB, LANES),
            buf(HALVES, row_blocks // HALVES, LANES), buf(HALVES, ncol, row_blocks // HALVES, LANES),
            buf(groups, LANES), buf(groups, LANES), buf(groups // 2, LANES),
            buf(chips, groups // 2, LANES), buf(groups, LANES), buf(groups, LANES),
            buf(groups, LANES), buf(groups, LANES), buf(groups // 2, LANES),
            buf(chips, groups // 2, LANES), buf(groups, LANES),
            buf(rows, width),
            buf(rows // ROWS5, ncol, ROWS5 // ncol, width), buf(rows, width),
            pltpu.SemaphoreType.DMA((42,)),
            pltpu.SemaphoreType.DMA((42,)),
            pltpu.SemaphoreType.DMA((cols // TILE0,)),
        ],
        compiler_params=pltpu.CompilerParams(
            collective_id=0, has_side_effects=True, vmem_limit_bytes=56 * 2**20
        ),
        name="sinkhorn",
    )(gen_points, ref_points, gen_mass.reshape(row_blocks, LANES), ref_mass.reshape(groups, LANES))
    f, g, grad = hand_on(f, g, grad)
    return f.reshape(rows), g.reshape(cols), grad


def solution(mesh):
    nrow, ncol = mesh.shape["row"], mesh.shape["col"]

    def run(*args):
        return local(nrow, ncol, *args)

    return jax.shard_map(
        run,
        mesh=mesh,
        in_specs=(P("row", None), P("col", None), P("row"), P("col")),
        out_specs=(P("row"), P("col"), P("row", None)),
        check_vma=False,
    )
```

```python
import math

import jax
import jax.numpy as jnp
from jax import lax
from jax.experimental import pallas as pl
from jax.experimental.pallas import tpu as pltpu
from jax.sharding import PartitionSpec as P

smoothing_epsilon = 0.05
SCALE = 1.0 / (smoothing_epsilon * math.log(2.0))
LANES = 128
SUB = 8
LOWEST = -3.0e38
f32 = jnp.float32
MESH = pl.DeviceIdType.MESH

CHUNK = 64
TILE0 = 2048
TILE1 = 4096
TILE2 = 4096
WIDE = 16
GROUPS3 = 16
GROUPS4 = 8
TILE5 = 2048
ROWS5 = 128
PARTS = 4
HALVES = 2


def scores(a, b):
    return lax.dot_general(a, b, (((1,), (1,)), ((), ())), preferred_element_type=f32)


def lane_cols(group):
    return pl.ds(pl.multiple_of(group * LANES, LANES), LANES)


def tile_rows(t):
    return pl.ds(pl.multiple_of(t * SUB, SUB), SUB)


def total(v):
    return jnp.sum(jnp.sum(v, axis=0, keepdims=True), axis=1, keepdims=True)


def log_sum(v):
    top = jnp.max(v, axis=0)
    return top + jnp.log2(jnp.sum(jnp.exp2(v - top[None]), axis=0))


def kernel(
    nrow, ncol, x, y_hbm, gm, rm, f_out, g_out, grad_out,
    y, R, MH, W, TOP, SUM, beta, acc_a, acc_b, lanes_u, row_f,
    sa, ra, ca, ta, zs1, zr1, zs3, zr3,
    cs2, cr2, gs2, ag2, col2, colw, cs4, cr4, gs4, ag4, col4,
    part, pr5, done, send_sem, recv_sem, load_sem,
):
    rows, width = x.shape
    cols = y.shape[0]
    loads = [
        pltpu.make_async_copy(
            y_hbm.at[pl.ds(t * TILE0, TILE0)], y.at[pl.ds(t * TILE0, TILE0)], load_sem.at[t]
        )
        for t in range(cols // TILE0)
    ]
    for load in loads:
        load.start()
    row_blocks = rows // LANES
    groups = cols // LANES
    tiles = groups // SUB
    half_tiles = tiles // 2
    half_groups = groups // 2
    chips = nrow // 2
    part_rows = rows // PARTS
    part_chunks = part_rows // CHUNK
    half_rows = rows // HALVES
    half_blocks = half_rows // LANES
    half_chunks = half_rows // CHUNK
    r = lax.axis_index("row")
    c = lax.axis_index("col")
    core = lax.rem(r, 2)
    chip = r // 2
    partner = 2 * chip + (1 - core)
    own = core * half_tiles
    other = (1 - core) * half_tiles

    def chip_peer(s):
        return lax.rem(r + 2 * s, nrow)

    def col_peer(s):
        return lax.rem(c + s, ncol)

    col_order = sorted(range(1, ncol), key=lambda s: -min(s, ncol - s))
    side = math.isqrt(chips)
    chip_order = sorted(
        range(1, chips),
        key=lambda s: -(min(s // side, side - s // side) + min(s % side, side - s % side)),
    )

    barrier = pltpu.get_barrier_semaphore()

    def greet_row(s, carry):
        pl.semaphore_signal(barrier, inc=1, device_id={"row": chip_peer(s)}, device_id_type=MESH)
        return carry

    def greet_col(s, carry):
        pl.semaphore_signal(barrier, inc=1, device_id={"col": col_peer(s)}, device_id_type=MESH)
        return carry

    pl.semaphore_signal(barrier, inc=1, device_id={"row": partner}, device_id_type=MESH)
    lax.fori_loop(1, chips, greet_row, 0)
    lax.fori_loop(1, ncol, greet_col, 0)

    def send(phase, device, source, target):
        pltpu.make_async_remote_copy(
            src_ref=source,
            dst_ref=target,
            send_sem=send_sem.at[phase],
            recv_sem=recv_sem.at[phase],
            device_id=device,
            device_id_type=MESH,
        ).start()

    def to_chips(phase, source, target):
        def one(s, carry):
            send(phase, {"row": chip_peer(s)}, source, target)
            return carry

        for s in chip_order:
            one(s, 0)

    def to_cols(phase, source, target):
        def one(s, carry):
            k = col_peer(s)
            send(phase, {"col": k}, source(k), target)
            return carry

        for s in col_order:
            one(s, 0)

    def arrived(phase, whole):
        pltpu.make_async_copy(whole, whole, recv_sem.at[phase]).wait()

    def left(phase, whole):
        pltpu.make_async_copy(whole, whole, send_sem.at[phase]).wait()

    Z1, Z3, CORE2, CHIP2, BACK2, CORE4, CHIP4, BACK4, A1, A2, RS, AG = (
        0, 4, 6, 10, 14, 15, 19, 23, 24, 25, 26, 34,
    )

    log_ref = jnp.log2(rm[...])
    beta[...] = log_ref
    zs1[...] = jnp.broadcast_to(total(rm[...])[None], zs1.shape)
    sa[...] = jnp.broadcast_to(total(gm[...]), sa.shape)
    acc_a[...] = jnp.full(acc_a.shape, LOWEST, f32)
    acc_b[...] = jnp.zeros(acc_b.shape, f32)
    TOP[...] = jnp.full(TOP.shape, LOWEST, f32)
    SUM[...] = jnp.zeros(SUM.shape, f32)

    def pass1(base, block, g0):
        rows_now = pl.ds(pl.multiple_of(base, part_rows), part_rows)
        tops, sums = acc_a.at[rows_now], acc_b.at[rows_now]
        for b in range(0, block.shape[1] // LANES, WIDE):
            bias = [beta[pl.ds(g0 + b + k, 1), :] for k in range(WIDE)]
            for i in range(0, part_rows, SUB):
                at = slice(i, i + SUB)
                e = [block[i:i + SUB, (b + k) * LANES:(b + k + 1) * LANES] * SCALE + bias[k] for k in range(WIDE)]
                old = tops[at, :]
                top = e[0]
                for v in e[1:]:
                    top = jnp.maximum(top, v)
                top = jnp.maximum(top, old)
                total_s = sums[at, :] * jnp.exp2(old - top)
                for v in e:
                    total_s = total_s + jnp.exp2(v - top)
                tops[at, :] = top
                sums[at, :] = total_s

    def report(h):
        o = pl.ds(pl.multiple_of(h * part_rows, part_rows), LANES)
        v = (acc_a[o, :] + jnp.log2(acc_b[o, :])).T
        top = jnp.max(v, axis=0, keepdims=True)
        zs1[h, 0:1, :] = top + jnp.log2(jnp.sum(jnp.exp2(v - top), axis=0, keepdims=True))

    def tell(h):
        to_cols(Z1 + h, lambda k: zs1.at[h], zr1.at[h, c])
        zr1[h, c] = zs1[h]

    n0 = TILE0 // LANES
    for t in range(cols // TILE0):
        loads[t].wait()
        points = y[t * TILE0:(t + 1) * TILE0, :]
        block = scores(x[0:part_rows, :], points)
        for k in range(n0):
            wide = points[k * LANES:(k + 1) * LANES, :].astype(f32)
            half = jnp.sum((wide * wide).T, axis=0, keepdims=True)
            g = t * n0 + k
            beta[g:g + 1, :] = beta[g:g + 1, :] - (0.5 * SCALE) * half
        pass1(0, block, t * n0)
    report(0)
    pl.semaphore_wait(barrier, chips + ncol - 1)
    tell(0)
    send(A1, {"row": partner}, sa, ra)

    n1 = TILE1 // LANES

    def pass1_part(h, carry):
        base = pl.multiple_of(h * part_rows, part_rows)

        def tile(t, carry):
            block = scores(x[pl.ds(base, part_rows), :], y[pl.ds(pl.multiple_of(t * TILE1, TILE1), TILE1), :])
            pass1(base, block, t * n1)
            return carry

        lax.fori_loop(0, cols // TILE1, tile, 0, unroll=True)
        report(h)
        tell(h)
        return carry

    lax.fori_loop(1, PARTS, pass1_part, 0)

    n2 = TILE2 // LANES
    t2 = n2 // SUB

    def spread(at, v):
        lanes_u[at, :] = jnp.broadcast_to(v, (LANES, LANES)).T

    def pass2(h, g0, last):
        base = pl.multiple_of(h * part_rows, part_rows)
        here = pl.ds(pl.multiple_of(g0 * LANES, TILE2), TILE2)
        block = scores(x[pl.ds(base, part_rows), :], y[here, :])
        powers = R.at[pl.ds(base, part_rows), here]
        u = lanes_u.at[pl.ds(base, part_rows)]
        marks = MH.at[pl.ds(pl.multiple_of(h * (part_chunks * SUB), SUB), part_chunks * SUB), here]
        top_now, sum_now = TOP.at[:, here], SUM.at[:, here]
        for b in range(0, n2, WIDE):
            cols_of = [slice(k * LANES, (k + 1) * LANES) for k in range(b, b + WIDE)]
            tops = [top_now[:, at] for at in cols_of]
            sums = [sum_now[:, at] for at in cols_of]
            bias = [beta[pl.ds(g0 + k, 1), :] for k in range(b, b + WIDE)]
            for j, at in enumerate(cols_of):
                top, s = tops[j], sums[j]
                for q in range(part_chunks):
                    span = range(q * CHUNK, (q + 1) * CHUNK, SUB)
                    e = [block[i:i + SUB, at] * SCALE + u[i:i + SUB, :] for i in span]
                    old = top
                    for v in e:
                        top = jnp.maximum(top, v)
                    s = s * jnp.exp2(old - top)
                    for i, v in zip(span, e):
                        z = jnp.exp2(v - top)
                        powers[i:i + SUB, at] = z
                        s = s + z
                    marks[q * SUB:(q + 1) * SUB, at] = top + bias[j]
                tops[j], sums[j] = top, s
            for j, at in enumerate(cols_of):
                if last:
                    best = jnp.max(tops[j], axis=0, keepdims=True)
                    s = jnp.sum(sums[j] * jnp.exp2(tops[j] - best), axis=0, keepdims=True)
                    cs2[pl.ds(g0 + b + j, 1), :] = best + jnp.log2(s) + bias[j]
                else:
                    top_now[:, at] = tops[j]
                    sum_now[:, at] = sums[j]

    def log_of_rows(h):
        arrived(Z1 + h, zr1.at[h, pl.ds(0, ncol - 1)])
        v = zr1[h]
        ref_total = jnp.sum(v, axis=0)[1:2, :]
        row_lse = log_sum(v)[0:1, :] - jnp.log2(ref_total)
        row_f[pl.ds(h, 1), :] = row_lse
        spread(pl.ds(pl.multiple_of(h * part_rows, part_rows), part_rows), jnp.log2(gm[pl.ds(h, 1), :]) - row_lse)
        return ref_total

    def pass2_part(h, carry):
        log_of_rows(h)

        def tile(t, carry):
            pass2(h, t * n2, False)
            return carry

        lax.fori_loop(0, groups // n2, tile, 0, unroll=True)
        return carry

    lax.fori_loop(0, PARTS - 1, pass2_part, 0)
    arrived(A1, ra)
    ca[...] = sa[...] + ra[...]
    to_chips(A2, ca, ta.at[chip])
    ta[chip] = ca[...]
    ref_total = log_of_rows(PARTS - 1)
    shares = jnp.log2(rm[...]) - jnp.log2(ref_total)

    def pass2_other(t, carry):
        g0 = other * SUB + t * n2
        pass2(PARTS - 1, g0, True)
        for j in range(t2):
            at = tile_rows(other + t * t2 + j)
            send(CORE2 + t * t2 + j, {"row": partner}, cs2.at[at], cr2.at[at])
        return carry

    def pass2_own(t, carry):
        g0 = own * SUB + t * n2
        pass2(PARTS - 1, g0, True)
        for j in range(t2):
            at = tile_rows(own + t * t2 + j)
            mine = tile_rows(t * t2 + j)
            arrived(CORE2 + t * t2 + j, cr2.at[at])
            a, b = cs2[at, :], cr2[at, :]
            top = jnp.maximum(a, b)
            both = top + jnp.log2(jnp.exp2(a - top) + jnp.exp2(b - top))
            gs2[mine, :] = both
            ag2[chip, mine, :] = both
            to_chips(CHIP2 + t * t2 + j, gs2.at[mine], ag2.at[chip, mine])
        return carry

    lax.fori_loop(0, half_groups // n2, pass2_other, 0)
    lax.fori_loop(0, half_groups // n2, pass2_own, 0)

    for j in range(half_tiles):
        mine = slice(j * SUB, (j + 1) * SUB)
        arrived(CHIP2 + j, ag2.at[pl.ds(0, chips - 1), mine])
        col2[tile_rows(own + j), :] = log_sum(ag2[:, mine, :])
    own_groups = pl.ds(pl.multiple_of(own * SUB, SUB), half_groups)
    other_groups = pl.ds(pl.multiple_of(other * SUB, SUB), half_groups)
    send(BACK2, {"row": partner}, col2.at[own_groups], col2.at[own_groups])
    colw[...] = -shares

    def weigh(half):
        colw[half, :] = col2[half, :] + colw[half, :]

    def pass3(first, h):
        def tile(t, carry):
            g0 = first * SUB + t * GROUPS3
            here = pl.ds(pl.multiple_of(g0 * LANES, GROUPS3 * LANES), GROUPS3 * LANES)
            powers, marks, weights = R.at[:, here], MH.at[:, here], W.at[:, here]
            cols_of = [slice(k * LANES, (k + 1) * LANES) for k in range(GROUPS3)]
            shift = [colw[pl.ds(g0 + k, 1), :] for k in range(GROUPS3)]
            for q in range(half_chunks):
                hq = (h * half_chunks + q) * SUB
                w = []
                for k, at in enumerate(cols_of):
                    v = jnp.exp2(marks[hq:hq + SUB, at] - shift[k])
                    weights[hq:hq + SUB, at] = v
                    w.append(v)
                for i in range(h * half_rows + q * CHUNK, h * half_rows + (q + 1) * CHUNK, SUB):
                    even = acc_a[i:i + SUB, :]
                    odd = jnp.zeros((SUB, LANES), f32)
                    for k, at in enumerate(cols_of):
                        v = powers[i:i + SUB, at] * w[k]
                        if k % 2:
                            odd = odd + v
                        else:
                            even = even + v
                    acc_a[i:i + SUB, :] = even + odd
            return carry

        lax.fori_loop(0, half_groups // GROUPS3, tile, 0)

    acc_a[...] = jnp.zeros(acc_a.shape, f32)
    weigh(own_groups)
    for h in range(HALVES):
        pass3(own, h)
    arrived(BACK2, col2.at[other_groups])
    weigh(other_groups)
    for h in range(HALVES):
        pass3(other, h)
        for k in range(half_blocks):
            o = (h * half_blocks + k) * LANES
            zs3[h, k:k + 1, :] = jnp.sum(acc_a[o:o + LANES, :].T, axis=0, keepdims=True)
        to_cols(Z3 + h, lambda k: zs3.at[h], zr3.at[h, c])
        zr3[h, c] = zs3[h]

    def pass4(h, g0):
        here = pl.ds(pl.multiple_of(g0 * LANES, GROUPS4 * LANES), GROUPS4 * LANES)
        powers, weights, partial = R.at[:, here], W.at[:, here], SUM.at[:, here]
        cols_of = [slice(k * LANES, (k + 1) * LANES) for k in range(GROUPS4)]
        sums = [partial[:, at] if h else jnp.zeros((SUB, LANES), f32) for at in cols_of]
        for q in range(half_chunks):
            hq = (h * half_chunks + q) * SUB
            inner = [jnp.zeros((SUB, LANES), f32) for _ in range(GROUPS4)]
            for i in range(h * half_rows + q * CHUNK, h * half_rows + (q + 1) * CHUNK, SUB):
                a = lanes_u[i:i + SUB, :]
                for k, at in enumerate(cols_of):
                    inner[k] = inner[k] + powers[i:i + SUB, at] * a
            for k, at in enumerate(cols_of):
                sums[k] = sums[k] + inner[k] * weights[hq:hq + SUB, at]
        for k, at in enumerate(cols_of):
            if h < HALVES - 1:
                partial[:, at] = sums[k]
            else:
                cs4[pl.ds(g0 + k, 1), :] = jnp.sum(sums[k], axis=0, keepdims=True)

    def scale_rows(h):
        arrived(Z3 + h, zr3.at[h, pl.ds(0, ncol - 1)])
        block = slice(h * half_blocks, (h + 1) * half_blocks)
        u = gm[block, :] / jnp.sum(zr3[h], axis=0)
        for k in range(half_blocks):
            o = (h * half_blocks + k) * LANES
            spread(slice(o, o + LANES), u[k:k + 1, :])
        row_f[block, :] = jnp.log2(u) - row_f[block, :]

    for h in range(HALVES - 1):
        scale_rows(h)

        def pass4_tile(t, carry, h=h):
            pass4(h, t * GROUPS4)
            return carry

        lax.fori_loop(0, groups // GROUPS4, pass4_tile, 0)
    scale_rows(HALVES - 1)

    def pass4_other(j, carry):
        for k in range(SUB // GROUPS4):
            pass4(HALVES - 1, (other + j) * SUB + k * GROUPS4)
        at = tile_rows(other + j)
        send(CORE4 + j, {"row": partner}, cs4.at[at], cr4.at[at])
        return carry

    def pass4_own(j, carry):
        for k in range(SUB // GROUPS4):
            pass4(HALVES - 1, (own + j) * SUB + k * GROUPS4)
        at = tile_rows(own + j)
        mine = tile_rows(j)
        arrived(CORE4 + j, cr4.at[at])
        both = cs4[at, :] + cr4[at, :]
        gs4[mine, :] = both
        ag4[chip, mine, :] = both
        to_chips(CHIP4 + j, gs4.at[mine], ag4.at[chip, mine])
        return carry

    lax.fori_loop(0, half_tiles, pass4_other, 0)
    lax.fori_loop(0, half_tiles, pass4_own, 0)

    arrived(A2, ta.at[pl.ds(0, chips - 1)])
    log_total = jnp.log2(jnp.sum(ta[...], axis=0)[0:1, :])
    for k in range(row_blocks):
        wide = x[k * LANES:(k + 1) * LANES, :].astype(f32)
        half = 0.5 * jnp.sum((wide * wide).T, axis=0, keepdims=True)
        f_out[k:k + 1, :] = half + (row_f[k:k + 1, :] - log_total) * (1.0 / SCALE)
    lanes_u[...] = lanes_u[...] * float(rows * nrow)
    acc_a[...] = jnp.zeros(acc_a.shape, f32)

    for j in range(half_tiles):
        mine = slice(j * SUB, (j + 1) * SUB)
        at = tile_rows(own + j)
        arrived(CHIP4 + j, ag4.at[pl.ds(0, chips - 1), mine])
        col4[at, :] = rm[at, :] / (ref_total * jnp.sum(ag4[:, mine, :], axis=0))
    send(BACK4, {"row": partner}, col4.at[own_groups], col4.at[own_groups])

    n5 = TILE5 // LANES
    share = ROWS5 // ncol

    def pass5(b, first):
        base = pl.multiple_of(b * ROWS5, ROWS5)
        whole = pl.ds(base, ROWS5)
        u, masses = lanes_u.at[whole], acc_a.at[whole]
        chunks_here = ROWS5 // CHUNK
        weight_rows = pl.ds(pl.multiple_of(b * (chunks_here * SUB), SUB), chunks_here * SUB)
        pulled = jnp.zeros((ROWS5, width), f32)
        in_half = half_groups // n5
        for t in range(2 * in_half):
            if first and t == in_half:
                arrived(BACK4, col4.at[other_groups])
            g0 = (own if t < in_half else other) * SUB + (t % in_half) * n5
            here = pl.ds(pl.multiple_of(g0 * LANES, TILE5), TILE5)
            powers, weights = R.at[whole, here], W.at[weight_rows, here]
            ratios = col4.at[pl.ds(pl.multiple_of(g0, SUB), n5)]
            low = [[] for _ in range(n5)]
            for q in range(ROWS5 // CHUNK):
                hq = slice(q * SUB, (q + 1) * SUB)
                w = [weights[hq, k * LANES:(k + 1) * LANES] * ratios[k:k + 1, :]
                     for k in range(n5)]
                for i in range(q * CHUNK, (q + 1) * CHUNK, SUB):
                    at = slice(i, i + SUB)
                    a = u[at, :]
                    mass = masses[at, :]
                    for k in range(n5):
                        p = (powers[at, k * LANES:(k + 1) * LANES] * w[k]) * a
                        mass = mass + p
                        low[k].append(p)
                    masses[at, :] = mass
            plan_low = jnp.concatenate(
                [jnp.concatenate(v, axis=0).astype(jnp.bfloat16) for v in low], axis=1
            )
            pulled = pulled + jnp.dot(plan_low, y[here, :], preferred_element_type=f32)
        mass_row = jnp.sum(masses[...], axis=1, keepdims=True)
        part[whole, :] = mass_row * x[whole, :].astype(f32) - pulled
        to_cols(
            RS + b,
            lambda k: part.at[pl.ds(pl.multiple_of(base + k * share, share), share)],
            pr5.at[b, c],
        )
        pr5[b, c] = part[pl.ds(pl.multiple_of(base + c * share, share), share), :]

    def pass5_later(b, carry):
        pass5(b, False)
        return carry

    pass5(0, True)
    lax.fori_loop(1, rows // ROWS5, pass5_later, 0)

    for j in range(tiles):
        at = slice(j * SUB, (j + 1) * SUB)
        g_out[at, :] = (
            (2.0 * log_total + jnp.log2(rm[at, :]) - col2[at, :]) + jnp.log2(col4[at, :])
        ) * (1.0 / SCALE)

    def finish(b, carry):
        mine = pl.ds(pl.multiple_of(b * ROWS5 + c * share, share), share)
        arrived(RS + b, pr5.at[b, pl.ds(0, ncol - 1)])
        done[mine, :] = jnp.sum(pr5[b], axis=0)
        to_cols(AG + b, lambda k: done.at[mine], done.at[mine])
        return carry

    lax.fori_loop(0, rows // ROWS5, finish, 0)
    for b in range(rows // ROWS5):
        arrived(AG + b, done.at[pl.ds(0, ROWS5 - share)])
    grad_out[...] = done[...]

    for h in range(PARTS):
        left(Z1 + h, zr1.at[h, pl.ds(0, ncol - 1)])
    for h in range(HALVES):
        left(Z3 + h, zr3.at[h, pl.ds(0, ncol - 1)])
    left(A1, ra)
    left(A2, ta.at[pl.ds(0, chips - 1)])
    for j in range(half_tiles):
        mine = slice(j * SUB, (j + 1) * SUB)
        left(CORE2 + j, cs2.at[mine])
        left(CORE4 + j, cs4.at[mine])
        left(CHIP2 + j, ag2.at[pl.ds(0, chips - 1), mine])
        left(CHIP4 + j, ag4.at[pl.ds(0, chips - 1), mine])
    left(BACK2, col2.at[own_groups])
    left(BACK4, col4.at[own_groups])
    for b in range(rows // ROWS5):
        left(RS + b, pr5.at[b, pl.ds(0, ncol - 1)])
        left(AG + b, done.at[pl.ds(0, ROWS5 - share)])


def move(f, g, grad, f_out, g_out, grad_out):
    f_out[...] = f[...]
    g_out[...] = g[...]
    grad_out[...] = grad[...]


def hand_on(*arrays):
    vmem = pl.BlockSpec(memory_space=pltpu.VMEM)
    return pl.pallas_call(
        move,
        out_shape=tuple(jax.ShapeDtypeStruct(a.shape, a.dtype) for a in arrays),
        in_specs=[vmem] * 3,
        out_specs=(vmem,) * 3,
        name="hand_on",
    )(*arrays)


def local(nrow, ncol, gen_points, ref_points, gen_mass, ref_mass):
    rows, width = gen_points.shape
    cols = ref_points.shape[0]
    row_blocks = rows // LANES
    groups = cols // LANES
    chunks = rows // CHUNK
    chips = nrow // 2
    vmem = pl.BlockSpec(memory_space=pltpu.VMEM)
    anywhere = pl.BlockSpec(memory_space=pl.ANY)

    def buf(*shape):
        return pltpu.VMEM(shape, f32)

    def body(*refs):
        kernel(nrow, ncol, *refs)

    f, g, grad = pl.pallas_call(
        body,
        out_shape=(
            jax.ShapeDtypeStruct((row_blocks, LANES), f32),
            jax.ShapeDtypeStruct((groups, LANES), f32),
            jax.ShapeDtypeStruct((rows, width), f32),
        ),
        in_specs=[vmem, anywhere, vmem, vmem],
        out_specs=(vmem, vmem, vmem),
        scratch_shapes=[
            pltpu.VMEM((cols, width), ref_points.dtype), buf(rows, cols), buf(chunks * SUB, cols), buf(chunks * SUB, cols), buf(SUB, cols), buf(SUB, cols), buf(groups, LANES),
            buf(rows, LANES), buf(rows, LANES), buf(rows, LANES), buf(row_blocks, LANES),
            buf(SUB, LANES), buf(SUB, LANES), buf(SUB, LANES), buf(chips, SUB, LANES),
            buf(PARTS, SUB, LANES), buf(PARTS, ncol, SUB, LANES),
            buf(HALVES, row_blocks // HALVES, LANES), buf(HALVES, ncol, row_blocks // HALVES, LANES),
            buf(groups, LANES), buf(groups, LANES), buf(groups // 2, LANES),
            buf(chips, groups // 2, LANES), buf(groups, LANES), buf(groups, LANES),
            buf(groups, LANES), buf(groups, LANES), buf(groups // 2, LANES),
            buf(chips, groups // 2, LANES), buf(groups, LANES),
            buf(rows, width),
            buf(rows // ROWS5, ncol, ROWS5 // ncol, width), buf(rows, width),
            pltpu.SemaphoreType.DMA((42,)),
            pltpu.SemaphoreType.DMA((42,)),
            pltpu.SemaphoreType.DMA((cols // TILE0,)),
        ],
        compiler_params=pltpu.CompilerParams(
            collective_id=0, has_side_effects=True, vmem_limit_bytes=56 * 2**20
        ),
        name="sinkhorn",
    )(gen_points, ref_points, gen_mass.reshape(row_blocks, LANES), ref_mass.reshape(groups, LANES))
    f, g, grad = hand_on(f, g, grad)
    return f.reshape(rows), g.reshape(cols), grad


def solution(mesh):
    nrow, ncol = mesh.shape["row"], mesh.shape["col"]

    def run(*args):
        return local(nrow, ncol, *args)

    return jax.shard_map(
        run,
        mesh=mesh,
        in_specs=(P("row", None), P("col", None), P("row"), P("col")),
        out_specs=(P("row"), P("col"), P("row", None)),
        check_vma=False,
    )
```
